128 devices in a mesh: group: 8 (over z, core), tile: 16 (over y, x).
Axes of the slice: x: 4, y: 4, z: 4, core: 2. Of those that a mesh axis runs over, the one named last changes fastest.
Arguments:
- embeddings: float32 [32768, 512], P(('group', 'tile'))
- cluster_ids: int32 [32768, 1], P(('group', 'tile')), may hold values from 0 to 7; in each aligned block of 256 rows (0 to 255, 256 to 511, ...) at most 96 rows name the same one
- order_rank: int32 [32768], P(('group', 'tile')), may hold values from 0 to 32767, each once
Outputs:
- nearest_earlier: float32 [32768], P(('group', 'tile'))
The draws below stay inside these ranges and needn't reach their ends.
Inputs may be any that keep to these rules, and one draw needn't show every extreme that they name: `cluster_ids`: in the rows of one device at most 96 name one cluster; some device has exactly 96 rows in one cluster. `order_rank`: all values differ.
All inputs are finite; a program needn't handle non-finite values.
Results may differ from the reference program's by a relative error of at most 0.00074.
Values may be sent and summed in bfloat16 or wider, within the bound.
No kernel may reach another device: no remote copies, remote signals or barrier semaphores. Data moves between devices by JAX's collectives and lax.ppermute only.
A program may use at most 64 MiB of HBM per device.

```python
import math
import jax
import jax.numpy as jnp
import numpy as np
from jax import lax

E = 512
ROWS_DEV = 256
CAP = 96
CLUSTERS = 8
ROWS = 32768


def draw_embeddings(key, part):
    key = jax.random.fold_in(key, 11)
    first = jax.random.fold_in(key, 0)
    base = jax.random.normal(first, (ROWS, E), jnp.float32)
    partner = jnp.roll(base, ROWS // 3 + 1, axis=0)
    return base + 0.9 * partner


def assign_block(own_key, own, number, rows, amount, top, reach, lean):
    order = jax.random.permutation(own_key, amount)
    packed, common = load_shares(amount, rows * top, reach, lean, True), load_shares(amount, rows * top, reach, lean, False)
    places = jnp.arange(amount)

    def named(lengths, turn):
        used = int((lengths > 0).sum())
        fixed = max(1, used // 4)
        passed = fixed + (places - fixed + turn * (used - fixed)) % max(1, amount - fixed)
        return jnp.zeros((amount,), jnp.int32).at[order[jnp.where(places < fixed, places, passed)]].set(jnp.asarray(lengths, jnp.int32))

    lengths = jnp.where(number % 4 == 0, named(packed, number // 4), named(common, number - number // 4 - 1))
    mixed = jax.random.permutation(jax.random.fold_in(own, 3), amount)
    source_of, taker = mixed[0:amount // 2 * 2:2], mixed[1:amount // 2 * 2:2]
    room = jnp.minimum(lengths[source_of] - 1, reach - lengths[taker]) // 2
    room = jnp.where((source_of == order[0]) | (taker == order[0]) | (lengths[taker] == 0), 0, jnp.maximum(room, 0))
    passed = jax.random.randint(jax.random.fold_in(own, 4), (amount // 2,), 0, 1 << 20) % (room + 1)
    lengths = lengths.at[source_of].add(-passed).at[taker].add(passed)
    items = jnp.searchsorted(jnp.cumsum(lengths), jnp.arange(rows * top), side="right").astype(jnp.int32)
    grid = items.reshape(top, rows).T
    grid = grid[jax.random.permutation(jax.random.fold_in(own, 1), rows)]
    turn = jax.random.randint(jax.random.fold_in(own, 2), (rows, 1), 0, top)
    return jnp.take_along_axis(grid, (jnp.arange(top)[None, :] + turn) % top, axis=1)


def load_shares(count, total, bound, lean, full):
    portions = [(1 << 20) // math.isqrt(standing ** lean) + 1 for standing in range(1, count + 1)]
    largest = bound if full else min(bound, max(-(-total // count), total * portions[0] // sum(portions)))
    least = 1 if total - largest >= count - 1 else 0
    holding, spare = [largest] + [least] * (count - 1), total - largest - least * (count - 1)
    while spare > 0:
        movable = [i for i in range(1, count) if holding[i] < largest] or [i for i in range(1, count) if holding[i] < bound]
        mass, left = sum([portions[i] for i in movable]), spare
        for i in movable:
            addition = min(bound - holding[i], max(1, left * portions[i] // mass), spare)
            holding[i] = holding[i] + addition
            spare = spare - addition
    return np.array(holding)


def setup_inputs(seed: int = 0) -> dict:
    seeds = jax.random.split(jax.random.key(seed), 4)
    embeddings = draw_embeddings(jax.random.fold_in(seeds[3], 71), 0)
    cluster_ids_keys = jax.random.split(jax.random.fold_in(seeds[1], 1), ROWS // ROWS_DEV)
    cluster_ids_turns = jax.random.permutation(jax.random.fold_in(seeds[1], 3), ROWS // ROWS_DEV)
    cluster_ids = jax.vmap(lambda own, number: assign_block(jax.random.fold_in(seeds[1], 2), own, number, ROWS_DEV, CLUSTERS, 1, CAP, 2))(cluster_ids_keys, cluster_ids_turns).reshape((ROWS, 1))
    order_rank = jax.random.permutation(seeds[2], ROWS).astype(jnp.int32)
    return dict(embeddings=embeddings, cluster_ids=cluster_ids, order_rank=order_rank)


def reference(embeddings, cluster_ids, order_rank):
    sums = lax.optimization_barrier(jnp.sum(embeddings * embeddings, axis=1, keepdims=True))
    unit = (embeddings * lax.rsqrt(sums + 1e-06)).astype(jnp.bfloat16)
    keys = unit.astype(jnp.float32)
    labels = cluster_ids[:, 0]
    width = math.gcd(ROWS, 512)

    def one_block(index):
        start = (index * width).astype(jnp.int32)
        query = lax.dynamic_slice_in_dim(keys, start, width, 0)
        qlab = lax.dynamic_slice_in_dim(labels, start, width, 0)
        qrank = lax.dynamic_slice_in_dim(order_rank, start, width, 0)
        scores = jnp.dot(query, keys.T, precision=lax.Precision.HIGHEST, preferred_element_type=jnp.float32)
        allowed = (labels[None, :] == qlab[:, None]) & (order_rank[None, :] < qrank[:, None])
        return lax.optimization_barrier(jnp.max(jnp.where(allowed, scores, jnp.float32(-1.0)), axis=1))
    blocks = lax.map(one_block, jnp.arange(ROWS // width, dtype=jnp.int32))
    return blocks.reshape(ROWS)
```

```python
import functools

import jax
import jax.numpy as jnp
from jax import lax
from jax.experimental import pallas as pl
from jax.experimental.pallas import tpu as pltpu
from jax.sharding import PartitionSpec as P

AXES = ("group", "tile")
ROWS = 256
META = 16
PAY = ROWS + META
E = 512
LOW = -(2**31)
NEAR = (1, 0, 3, 2)
OTHER = (3, 2, 1, 0)
PLACES = [(x, y, z, c) for x in range(4) for y in range(4) for z in range(4) for c in range(2)]


def linear(x, y, z, c):
    return (z * 2 + c) * 16 + y * 4 + x


def across(place, mask, both):
    x, y, z, c = place
    step = OTHER if (c and both) else NEAR
    return (
        step[x] if mask & 1 else x,
        step[y] if mask & 2 else y,
        step[z] if mask & 4 else z,
        c,
    )


def exchange(array, mask):
    pairs = [(linear(*across(q, mask, True)), linear(*q)) for q in PLACES]
    return lax.ppermute(array, AXES, pairs)


def swap(array):
    pairs = [(linear(x, y, z, 1 - c), linear(x, y, z, c)) for x, y, z, c in PLACES]
    return lax.ppermute(array, AXES, pairs)


def cube_groups():
    groups = []
    for x, y, z, c in PLACES:
        if x % 2 == 0 and y % 2 == 0 and z % 2 == 0:
            groups.append([linear(x + (k & 1), y + (k >> 1 & 1), z + (k >> 2 & 1), c) for k in range(8)])
    return groups


def unit_kernel(emb_ref, cluster_ref, rank_ref, out_ref):
    emb = emb_ref[...]
    sums = jnp.sum(emb * emb, axis=1, keepdims=True)
    out_ref[0:ROWS, :] = (emb * lax.rsqrt(sums + 1e-06)).astype(jnp.bfloat16)
    rank = rank_ref[...]
    high = (rank >> 8).astype(jnp.float32)
    low = (rank & 255).astype(jnp.float32)
    cluster = cluster_ref[...].astype(jnp.float32)
    first = jnp.concatenate([high, low], axis=1)
    second = jnp.concatenate([cluster, jnp.zeros_like(cluster)], axis=1)
    row = lax.broadcasted_iota(jnp.int32, (META, E), 0)
    meta = jnp.where(row == 0, first, jnp.where(row == 1, second, 0.0))
    out_ref[ROWS:PAY, :] = meta.astype(jnp.bfloat16)


def unit_rows(embeddings, cluster_ids, order_rank):
    return pl.pallas_call(
        unit_kernel,
        out_shape=jax.ShapeDtypeStruct((PAY, E), jnp.bfloat16),
        in_specs=[pl.BlockSpec(memory_space=pltpu.VMEM)] * 3,
        out_specs=pl.BlockSpec(memory_space=pltpu.VMEM),
        cost_estimate=pl.CostEstimate(flops=1000000, bytes_accessed=800000, transcendentals=256),
    )(embeddings, cluster_ids.reshape(1, ROWS), order_rank.reshape(1, ROWS))


def match_kernel(old, new, *refs):
    count = len(old) + len(new)
    masks = old + new
    others = [m for m in masks if m]
    scalar_ref, own_ref = refs[0], refs[1]
    mine = dict(zip(others, refs[2 : 2 + len(others)]))
    theirs = dict(zip(others, refs[2 + len(others) : 2 + 2 * len(others)]))
    rest = refs[2 + 2 * len(others) :]
    prev_ref, out_ref, qbuf, kbuf, qsem, ksem, qkey, qrank, kkey, acc = rest
    core, code = scalar_ref[0], scalar_ref[1]
    at = {m: i for i, m in enumerate(masks)}

    def query_copy(m, source):
        return pltpu.make_async_copy(source, qbuf.at[at[m]], qsem.at[at[m]])

    def key_copy(m, source):
        return pltpu.make_async_copy(source, kbuf.at[at[m]], ksem.at[at[m]])

    def start_query(m):
        if m == 0:
            query_copy(m, own_ref.at[0]).start()
            return

        @pl.when(core == 0)
        def _():
            query_copy(m, mine[m].at[0]).start()

        @pl.when(core == 1)
        def _():
            query_copy(m, theirs[m].at[1]).start()

    def start_key(m):
        if m == 0:
            key_copy(m, own_ref).start()
            return

        @pl.when(core == 0)
        def _():
            key_copy(m, theirs[m]).start()

        @pl.when(core == 1)
        def _():
            key_copy(m, mine[m]).start()

    for m in new:
        start_query(m)
    for m in masks:
        start_key(m)
    for m in old:
        start_query(m)

    def load_query(m):
        i = at[m]
        query_copy(m, own_ref.at[0]).wait()
        meta = qbuf[i, ROWS:PAY, :].astype(jnp.float32)
        rank = meta[0:1, 0:ROWS] * 256.0 + meta[0:1, ROWS : 2 * ROWS]
        key = meta[1:2, 0:ROWS] * 32768.0 + rank
        both = jnp.concatenate([key, rank, jnp.zeros((6, ROWS), jnp.float32)], axis=0)
        columns = jnp.transpose(both)
        qkey[i] = jnp.broadcast_to(columns[:, 0:1], (ROWS, 128)).astype(jnp.int32)
        qrank[i] = jnp.broadcast_to(columns[:, 1:2], (ROWS, 128)).astype(jnp.int32) + LOW
        acc[i] = jnp.full((ROWS, 128), -1.0, jnp.float32)

    def load_key(m):
        i = at[m]
        key_copy(m, own_ref).wait()
        for h in range(2):
            meta = kbuf[i, h, ROWS:PAY, :].astype(jnp.float32)
            rank = meta[0:1, 0:ROWS] * 256.0 + meta[0:1, ROWS : 2 * ROWS]
            key = meta[1:2, 0:ROWS] * 32768.0 + rank
            kkey[i, h] = key.astype(jnp.int32) + (LOW + 1)

    def rect(queries, keys):
        q0, k0 = at[queries[0]], at[keys[0]]
        nq, nk = len(queries), len(keys)

        def step(t, carry):
            k = k0 + t // 2
            h = t % 2
            tile = kbuf[k, h, 0:ROWS, :]
            row = kkey[k, h]
            for q in range(q0, q0 + nq):
                score = lax.dot_general(
                    qbuf[q, 0:ROWS, :], tile, (((1,), (1,)), ((), ())), preferred_element_type=jnp.float32
                )
                best = acc[q]
                for half in range(2):
                    lanes = slice(half * 128, half * 128 + 128)
                    gap = qkey[q] - row[:, lanes]
                    best = jnp.maximum(best, jnp.where(gap < qrank[q], score[:, lanes], -1.0))
                acc[q] = best
            return carry

        lax.fori_loop(0, nk * 2, step, 0)

    for m in new:
        load_query(m)
    for m in masks:
        load_key(m)
    for m in old:
        load_query(m)
    rect(new, masks)
    if old:
        rect(old, new)
    out_ref[...] = prev_ref[...]
    for m in masks:
        found = jnp.max(jnp.transpose(acc[at[m]]), axis=0, keepdims=True)
        slot = code ^ m
        out_ref[slot] = jnp.maximum(out_ref[slot], found)


def match(old, new, scalars, own, mine, theirs, prev):
    masks = old + new
    others = [m for m in masks if m]
    count = len(masks)
    pairs = len(new) * count + len(old) * len(new)
    anywhere = pl.BlockSpec(memory_space=pl.ANY)
    return pl.pallas_call(
        functools.partial(match_kernel, old, new),
        out_shape=jax.ShapeDtypeStruct((8, 1, ROWS), jnp.float32),
        in_specs=[pl.BlockSpec(memory_space=pltpu.SMEM)]
        + [anywhere] * (1 + 2 * len(others))
        + [pl.BlockSpec(memory_space=pltpu.VMEM)],
        out_specs=pl.BlockSpec(memory_space=pltpu.VMEM),
        scratch_shapes=[
            pltpu.VMEM((count, PAY, E), jnp.bfloat16),
            pltpu.VMEM((count, 2, PAY, E), jnp.bfloat16),
            pltpu.SemaphoreType.DMA((count,)),
            pltpu.SemaphoreType.DMA((count,)),
            pltpu.VMEM((count, ROWS, 128), jnp.int32),
            pltpu.VMEM((count, ROWS, 128), jnp.int32),
            pltpu.VMEM((count, 2, 1, ROWS), jnp.int32),
            pltpu.VMEM((count, ROWS, 128), jnp.float32),
        ],
        compiler_params=pltpu.CompilerParams(vmem_limit_bytes=40 * 2**20),
        cost_estimate=pl.CostEstimate(
            flops=pairs * 2 * ROWS * 2 * ROWS * E, bytes_accessed=count * 3 * PAY * E * 2, transcendentals=0
        ),
    )(scalars, own, *[mine[m] for m in others], *[theirs[m] for m in others], prev)


def on_device(embeddings, cluster_ids, order_rank):
    group, tile = lax.axis_index("group"), lax.axis_index("tile")
    core = group % 2
    code = (tile % 2) + 2 * (tile // 4 % 2) + 4 * (group // 2 % 2)
    scalars = jnp.stack([core, code]).astype(jnp.int32)
    unit = unit_rows(embeddings, cluster_ids, order_rank)
    own = jnp.stack([unit, swap(unit)])
    mine = {m: exchange(own, m) for m in (1, 2, 4)}
    mine[3] = exchange(mine[1], 2)
    mine[6] = exchange(mine[2], 4)
    mine[5] = exchange(mine[4], 1)
    theirs = {m: swap(mine[m]) for m in (1, 2, 4)}
    mine[7] = exchange(mine[3], 4)
    theirs.update({m: swap(mine[m]) for m in (3, 6, 5, 7)})
    best = jnp.full((8, 1, ROWS), -1.0, jnp.float32)
    best = match((), (0, 1, 2, 4), scalars, own, mine, theirs, best)
    best = match((0, 1, 2, 4), (3, 6, 5), scalars, own, mine, theirs, best)
    best = match((0, 1, 2, 4, 3, 6, 5), (7,), scalars, own, mine, theirs, best)
    back = lax.all_to_all(best, AXES, split_axis=0, concat_axis=0, axis_index_groups=cube_groups())
    return jnp.max(back, axis=0)[0]


def solution(mesh):
    return jax.shard_map(
        on_device,
        mesh=mesh,
        in_specs=(P(AXES, None), P(AXES, None), P(AXES)),
        out_specs=P(AXES),
        check_vma=False,
    )
```

```python
import functools

import jax
import jax.numpy as jnp
from jax import lax
from jax.experimental import pallas as pl
from jax.experimental.pallas import tpu as pltpu
from jax.sharding import PartitionSpec as P

AXES = ("group", "tile")
ROWS = 256
META = 16
PAY = ROWS + META
E = 512
LOW = -(2**31)
NEAR = (1, 0, 3, 2)
OTHER = (3, 2, 1, 0)
PLACES = [(x, y, z, c) for x in range(4) for y in range(4) for z in range(4) for c in range(2)]


def linear(x, y, z, c):
    return (z * 2 + c) * 16 + y * 4 + x


def across(place, mask):
    x, y, z, c = place
    step = OTHER if c else NEAR
    return (
        step[x] if mask & 1 else x,
        step[y] if mask & 2 else y,
        step[z] if mask & 4 else z,
        c,
    )


def exchange(array, mask):
    pairs = [(linear(*across(q, mask)), linear(*q)) for q in PLACES]
    return lax.ppermute(array, AXES, pairs)


def swap(array):
    pairs = [(linear(x, y, z, 1 - c), linear(x, y, z, c)) for x, y, z, c in PLACES]
    return lax.ppermute(array, AXES, pairs)


def cube_groups():
    groups = []
    for place in PLACES:
        starts = (0, 1) if place[3] else (0, 2)
        if all(p in starts for p in place[:3]):
            groups.append([linear(*across(place, k)) for k in range(8)])
    return groups


def unit_kernel(emb_ref, cluster_ref, rank_ref, out_ref):
    emb = emb_ref[...]
    sums = jnp.sum(emb * emb, axis=1, keepdims=True)
    out_ref[0:ROWS, :] = (emb * lax.rsqrt(sums + 1e-06)).astype(jnp.bfloat16)
    rank = rank_ref[...]
    high = (rank >> 8).astype(jnp.float32)
    low = (rank & 255).astype(jnp.float32)
    cluster = cluster_ref[...].astype(jnp.float32)
    first = jnp.concatenate([high, low], axis=1)
    second = jnp.concatenate([cluster, jnp.zeros_like(cluster)], axis=1)
    row = lax.broadcasted_iota(jnp.int32, (META, E), 0)
    meta = jnp.where(row == 0, first, jnp.where(row == 1, second, 0.0))
    out_ref[ROWS:PAY, :] = meta.astype(jnp.bfloat16)


def unit_rows(embeddings, cluster_ids, order_rank):
    return pl.pallas_call(
        unit_kernel,
        out_shape=jax.ShapeDtypeStruct((PAY, E), jnp.bfloat16),
        in_specs=[pl.BlockSpec(memory_space=pltpu.VMEM)] * 3,
        out_specs=pl.BlockSpec(memory_space=pltpu.VMEM),
        cost_estimate=pl.CostEstimate(flops=1000000, bytes_accessed=800000, transcendentals=256),
    )(embeddings, cluster_ids.reshape(1, ROWS), order_rank.reshape(1, ROWS))


def match_kernel(old, new, *refs):
    masks = old + new
    others = [m for m in masks if m]
    code_ref, own_ref = refs[0], refs[1]
    mine = dict(zip(others, refs[2 : 2 + len(others)]))
    theirs = dict(zip(others, refs[2 + len(others) : 2 + 2 * len(others)]))
    mine[0] = theirs[0] = own_ref
    prev_ref, out_ref, qkey, qrank, kkey = refs[2 + 2 * len(others) :]
    fresh = {m: i for i, m in enumerate(new)}

    def numbers(meta):
        meta = meta.astype(jnp.float32)
        rank = meta[0:1, 0:ROWS] * 256.0 + meta[0:1, ROWS : 2 * ROWS]
        return rank, meta[1:2, 0:ROWS] * 32768.0 + rank

    def columns(row):
        return jnp.broadcast_to(jnp.transpose(jnp.broadcast_to(row, (8, ROWS)))[:, 0:1], (ROWS, 128)).astype(jnp.int32)

    def product(left, right):
        return lax.dot_general(left, right, (((1,), (1,)), ((), ())), preferred_element_type=jnp.float32)

    code = code_ref[0]
    out_ref[...] = prev_ref[...]
    found = {}
    rows = {}
    for m in new:
        rank, key = numbers(mine[m][0, ROWS:PAY, :])
        qkey[fresh[m]] = columns(key)
        qrank[fresh[m]] = columns(rank) + LOW
    for m in masks:
        for h in range(2):
            key = numbers(theirs[m][h, ROWS:PAY, :])[1]
            rows[m, h] = key.astype(jnp.int32) + (LOW + 1)
            if old and m in new:
                kkey[fresh[m], h * ROWS : h * ROWS + ROWS, :] = columns(key) + (LOW + 1)
    for m in new:
        best = jnp.full((ROWS, 128), -1.0, jnp.float32)
        column, limit = qkey[fresh[m]], qrank[fresh[m]]
        for n in masks:
            for h in range(2):
                score = product(mine[m][0, 0:ROWS, :], theirs[n][h, 0:ROWS, :])
                for lanes in (slice(0, 128), slice(128, 256)):
                    valid = column - rows[n, h][:, lanes] < limit
                    best = jnp.maximum(best, jnp.where(valid, score[:, lanes], -1.0))
        found[m] = jnp.max(jnp.transpose(best), axis=0, keepdims=True)
    for m in old:
        rank, key = numbers(mine[m][0, ROWS:PAY, :])
        row = jnp.broadcast_to(key.astype(jnp.int32), (8, ROWS))
        limit = jnp.broadcast_to(rank.astype(jnp.int32) + LOW, (8, ROWS))
        best = jnp.full((8, ROWS), -1.0, jnp.float32)
        for n in new:
            for h in range(2):
                score = product(theirs[n][h, 0:ROWS, :], mine[m][0, 0:ROWS, :])
                for r in range(0, ROWS, 8):
                    column = kkey[fresh[n], h * ROWS + r : h * ROWS + r + 8, :]
                    valid = row - jnp.concatenate([column, column], axis=1) < limit
                    best = jnp.maximum(best, jnp.where(valid, score[r : r + 8, :], -1.0))
        found[m] = jnp.max(best, axis=0, keepdims=True)
    for m in masks:
        slot = code ^ m
        out_ref[slot] = jnp.maximum(out_ref[slot], found[m])


def match(old, new, code, own, mine, theirs, prev):
    masks = old + new
    others = [m for m in masks if m]
    count = len(masks)
    pairs = len(new) * count + len(old) * len(new)
    vmem = pl.BlockSpec(memory_space=pltpu.VMEM)
    return pl.pallas_call(
        functools.partial(match_kernel, old, new),
        out_shape=jax.ShapeDtypeStruct((8, 1, ROWS), jnp.float32),
        in_specs=[pl.BlockSpec(memory_space=pltpu.SMEM)] + [vmem] * (2 + 2 * len(others)),
        out_specs=vmem,
        scratch_shapes=[
            pltpu.VMEM((len(new), ROWS, 128), jnp.int32),
            pltpu.VMEM((len(new), ROWS, 128), jnp.int32),
            pltpu.VMEM((len(new), 2 * ROWS, 128), jnp.int32),
        ],
        compiler_params=pltpu.CompilerParams(vmem_limit_bytes=24 * 2**20),
        cost_estimate=pl.CostEstimate(
            flops=pairs * 2 * ROWS * 2 * ROWS * E, bytes_accessed=count * 3 * PAY * E * 2, transcendentals=0
        ),
    )(code, own, *[mine[m] for m in others], *[theirs[m] for m in others], prev)


def on_device(embeddings, cluster_ids, order_rank):
    group, tile = lax.axis_index("group"), lax.axis_index("tile")
    places = (tile % 4, tile // 4, group // 2)
    code = sum(jnp.where(group % 2 == 0, p % 2, p // 2) << i for i, p in enumerate(places))
    code = code.astype(jnp.int32).reshape(1)
    unit = unit_rows(embeddings, cluster_ids, order_rank)
    own = jnp.stack([unit, swap(unit)])
    best = jnp.full((8, 1, ROWS), -1.0, jnp.float32)
    mine = {m: exchange(own, m) for m in (1, 2, 4)}
    mine[3] = exchange(mine[1], 2)
    mine[6] = exchange(mine[2], 4)
    mine[5] = exchange(mine[4], 1)
    theirs = {m: swap(mine[m]) for m in (1, 2, 4)}
    best = match((), (0, 1, 2, 4), code, own, mine, theirs, best)
    mine[3], mine[6], mine[5], best = lax.optimization_barrier((mine[3], mine[6], mine[5], best))
    mine[7] = exchange(mine[3], 4)
    theirs.update({m: swap(mine[m]) for m in (3, 6, 5)})
    best = match((0, 1, 2, 4), (3, 6, 5), code, own, mine, theirs, best)
    mine[7], best = lax.optimization_barrier((mine[7], best))
    theirs[7] = swap(mine[7])
    best = match((0, 1, 2, 4, 3, 6, 5), (7,), code, own, mine, theirs, best)
    back = lax.all_to_all(best, AXES, split_axis=0, concat_axis=0, axis_index_groups=cube_groups())
    return jnp.max(back, axis=0)[0]


def solution(mesh):
    return jax.shard_map(
        on_device,
        mesh=mesh,
        in_specs=(P(AXES, None), P(AXES, None), P(AXES)),
        out_specs=P(AXES),
        check_vma=False,
    )
```

```python
import functools

import jax
import jax.numpy as jnp
from jax import lax
from jax.experimental import pallas as pl
from jax.experimental.pallas import tpu as pltpu
from jax.sharding import PartitionSpec as P

AXES = ("group", "tile")
ROWS = 256
META = 16
PAY = ROWS + META
E = 512
LOW = -(2**31)
GRANT = 12 * 2**20
NEAR = (1, 0, 3, 2)
OTHER = (3, 2, 1, 0)
PLACES = [(x, y, z, c) for x in range(4) for y in range(4) for z in range(4) for c in range(2)]


def linear(x, y, z, c):
    return (z * 2 + c) * 16 + y * 4 + x


def across(place, mask):
    x, y, z, c = place
    step = OTHER if c else NEAR
    return (
        step[x] if mask & 1 else x,
        step[y] if mask & 2 else y,
        step[z] if mask & 4 else z,
        c,
    )


def exchange(array, mask):
    pairs = [(linear(*across(q, mask)), linear(*q)) for q in PLACES]
    return lax.ppermute(array, AXES, pairs)


def swap(array):
    pairs = [(linear(x, y, z, 1 - c), linear(x, y, z, c)) for x, y, z, c in PLACES]
    return lax.ppermute(array, AXES, pairs)


def cube_groups():
    groups = []
    for place in PLACES:
        starts = (0, 1) if place[3] else (0, 2)
        if all(p in starts for p in place[:3]):
            groups.append([linear(*across(place, k)) for k in range(8)])
    return groups


def unit_kernel(*refs):
    out_ref = refs[-1]
    for h in range(2):
        emb_ref, cluster_ref, rank_ref = refs[3 * h : 3 * h + 3]
        emb = emb_ref[...]
        sums = jnp.sum(emb * emb, axis=1, keepdims=True)
        out_ref[h, 0:ROWS, :] = (emb * lax.rsqrt(sums + 1e-06)).astype(jnp.bfloat16)
        rank = rank_ref[...]
        high = (rank >> 8).astype(jnp.float32)
        low = (rank & 255).astype(jnp.float32)
        cluster = cluster_ref[...].astype(jnp.float32)
        first = jnp.concatenate([high, low], axis=1)
        second = jnp.concatenate([cluster, jnp.zeros_like(cluster)], axis=1)
        row = lax.broadcasted_iota(jnp.int32, (META, E), 0)
        meta = jnp.where(row == 0, first, jnp.where(row == 1, second, 0.0))
        out_ref[h, ROWS:PAY, :] = meta.astype(jnp.bfloat16)


def payload(*halves):
    vmem = pl.BlockSpec(memory_space=pltpu.VMEM)
    return pl.pallas_call(
        unit_kernel,
        out_shape=jax.ShapeDtypeStruct((2, PAY, E), jnp.bfloat16),
        in_specs=[vmem] * 6,
        out_specs=vmem,
        compiler_params=pltpu.CompilerParams(vmem_limit_bytes=GRANT),
        cost_estimate=pl.CostEstimate(flops=2000000, bytes_accessed=1600000, transcendentals=512),
    )(*halves)


def match_kernel(queries, keys, *refs):
    code_ref = refs[0]
    mine = dict(zip(queries, refs[1 : 1 + len(queries)]))
    theirs = dict(zip(keys, refs[1 + len(queries) : 1 + len(queries) + len(keys)]))
    prev_ref, out_ref, first, second = refs[1 + len(queries) + len(keys) :]

    def numbers(meta):
        meta = meta.astype(jnp.float32)
        rank = meta[0:1, 0:ROWS] * 256.0 + meta[0:1, ROWS : 2 * ROWS]
        return rank, meta[1:2, 0:ROWS] * 32768.0 + rank

    def columns(row):
        return jnp.broadcast_to(jnp.transpose(jnp.broadcast_to(row, (8, ROWS)))[:, 0:1], (ROWS, 128)).astype(jnp.int32)

    def product(left, right):
        return lax.dot_general(left, right, (((1,), (1,)), ((), ())), preferred_element_type=jnp.float32)

    found = {}
    sides = [(n, h) for n in keys for h in range(2)]
    limits = {m: numbers(mine[m][0, ROWS:PAY, :]) for m in queries}
    wanted = {(n, h): numbers(theirs[n][h, ROWS:PAY, :])[1] for n, h in sides}
    if len(queries) < len(keys):
        for i, m in enumerate(queries):
            first[i] = columns(limits[m][1])
            second[i] = columns(limits[m][0]) + LOW
        rows = {side: wanted[side].astype(jnp.int32) + (LOW + 1) for side in sides}
        for i, m in enumerate(queries):
            best = jnp.full((ROWS, 128), -1.0, jnp.float32)
            for n, h in sides:
                score = product(mine[m][0, 0:ROWS, :], theirs[n][h, 0:ROWS, :])
                for lanes in (slice(0, 128), slice(128, 256)):
                    valid = first[i] - rows[n, h][:, lanes] < second[i]
                    best = jnp.maximum(best, jnp.where(valid, score[:, lanes], -1.0))
            found[m] = jnp.max(jnp.transpose(best), axis=0, keepdims=True)
    else:
        for i, side in enumerate(sides):
            first[i] = columns(wanted[side]) + (LOW + 1)
        for m in queries:
            row = jnp.broadcast_to(limits[m][1].astype(jnp.int32), (8, ROWS))
            limit = jnp.broadcast_to(limits[m][0].astype(jnp.int32) + LOW, (8, ROWS))
            best = jnp.full((8, ROWS), -1.0, jnp.float32)
            for i, (n, h) in enumerate(sides):
                score = product(theirs[n][h, 0:ROWS, :], mine[m][0, 0:ROWS, :])
                for r in range(0, ROWS, 8):
                    column = first[i, r : r + 8, :]
                    valid = row - jnp.concatenate([column, column], axis=1) < limit
                    best = jnp.maximum(best, jnp.where(valid, score[r : r + 8, :], -1.0))
            found[m] = jnp.max(best, axis=0, keepdims=True)
    code = code_ref[0]
    out_ref[...] = prev_ref[...]
    for m in queries:
        slot = code ^ m
        out_ref[slot] = jnp.maximum(out_ref[slot], found[m])


def match(queries, keys, code, mine, theirs, prev):
    columns = len(queries) if len(queries) < len(keys) else 2 * len(keys)
    vmem = pl.BlockSpec(memory_space=pltpu.VMEM)
    return pl.pallas_call(
        functools.partial(match_kernel, queries, keys),
        out_shape=jax.ShapeDtypeStruct((8, 1, ROWS), jnp.float32),
        in_specs=[pl.BlockSpec(memory_space=pltpu.SMEM)] + [vmem] * (len(queries) + len(keys) + 1),
        out_specs=vmem,
        scratch_shapes=[pltpu.VMEM((columns, ROWS, 128), jnp.int32)] * 2,
        compiler_params=pltpu.CompilerParams(vmem_limit_bytes=GRANT),
        cost_estimate=pl.CostEstimate(
            flops=len(queries) * len(keys) * 2 * ROWS * 2 * ROWS * E, bytes_accessed=1000, transcendentals=0
        ),
    )(code, *[mine[m] for m in queries], *[theirs[m] for m in keys], prev)


def on_device(embeddings, cluster_ids, order_rank):
    group, tile = lax.axis_index("group"), lax.axis_index("tile")
    places = (tile % 4, tile // 4, group // 2)
    code = sum(jnp.where(group % 2 == 0, p % 2, p // 2) << i for i, p in enumerate(places))
    code = code.astype(jnp.int32).reshape(1)
    half = (embeddings, cluster_ids.reshape(1, ROWS), order_rank.reshape(1, ROWS))
    own = payload(*half, *[swap(part) for part in half])
    best = jnp.full((8, 1, ROWS), -1.0, jnp.float32)
    mine, theirs = {0: own}, {0: own}
    for m in (1, 2, 4):
        mine[m] = exchange(own, m)
    mine[3] = exchange(mine[1], 2)
    mine[6] = exchange(mine[2], 4)
    mine[5] = exchange(mine[4], 1)
    best = match((0, 1, 2, 4), (0,), code, mine, theirs, best)
    theirs.update({m: swap(mine[m]) for m in (1, 2, 4)})
    best = match((0, 1, 2, 4), (1, 2, 4), code, mine, theirs, best)
    mine[3], mine[6], mine[5], best = lax.optimization_barrier((mine[3], mine[6], mine[5], best))
    mine[7] = exchange(mine[3], 4)
    best = match((3, 6, 5), (0, 1, 2, 4), code, mine, theirs, best)
    theirs.update({m: swap(mine[m]) for m in (3, 6, 5)})
    best = match((0, 1, 2, 4, 3, 6, 5), (3, 6, 5), code, mine, theirs, best)
    mine[7], best = lax.optimization_barrier((mine[7], best))
    theirs[7] = swap(mine[7])
    best = match((7,), (0, 1, 2, 4, 3, 6, 5), code, mine, theirs, best)
    best = match((0, 1, 2, 4, 3, 6, 5, 7), (7,), code, mine, theirs, best)
    back = lax.all_to_all(best, AXES, split_axis=0, concat_axis=0, axis_index_groups=cube_groups())
    return jnp.max(back, axis=0)[0]


def solution(mesh):
    return jax.shard_map(
        on_device,
        mesh=mesh,
        in_specs=(P(AXES, None), P(AXES, None), P(AXES)),
        out_specs=P(AXES),
        check_vma=False,
    )
```

```python
import functools

import jax
import jax.numpy as jnp
from jax import lax
from jax.experimental import pallas as pl
from jax.experimental.pallas import tpu as pltpu
from jax.sharding import PartitionSpec as P

AXES = ("group", "tile")
ROWS = 256
META = 16
PAY = ROWS + META
E = 512
LOW = -(2**31)
GRANT = 12 * 2**20
NEAR = (1, 0, 3, 2)
OTHER = (3, 2, 1, 0)
PLACES = [(x, y, z, c) for x in range(4) for y in range(4) for z in range(4) for c in range(2)]


def linear(x, y, z, c):
    return (z * 2 + c) * 16 + y * 4 + x


def across(place, mask):
    x, y, z, c = place
    step = OTHER if c else NEAR
    return (
        step[x] if mask & 1 else x,
        step[y] if mask & 2 else y,
        step[z] if mask & 4 else z,
        c,
    )


def exchange(array, mask):
    pairs = [(linear(*across(q, mask)), linear(*q)) for q in PLACES]
    return lax.ppermute(array, AXES, pairs)


def swap(array):
    pairs = [(linear(x, y, z, 1 - c), linear(x, y, z, c)) for x, y, z, c in PLACES]
    return lax.ppermute(array, AXES, pairs)


def cube_groups():
    groups = []
    for place in PLACES:
        starts = (0, 1) if place[3] else (0, 2)
        if all(p in starts for p in place[:3]):
            groups.append([linear(*across(place, k)) for k in range(8)])
    return groups


def unit_kernel(*refs):
    out_ref = refs[-1]
    for h in range(2):
        emb_ref, cluster_ref, rank_ref = refs[3 * h : 3 * h + 3]
        emb = emb_ref[...]
        sums = jnp.sum(emb * emb, axis=1, keepdims=True)
        out_ref[h, 0:ROWS, :] = (emb * lax.rsqrt(sums + 1e-06)).astype(jnp.bfloat16)
        rank = rank_ref[...]
        high = (rank >> 8).astype(jnp.float32)
        low = (rank & 255).astype(jnp.float32)
        cluster = cluster_ref[...].astype(jnp.float32)
        first = jnp.concatenate([high, low], axis=1)
        second = jnp.concatenate([cluster, jnp.zeros_like(cluster)], axis=1)
        row = lax.broadcasted_iota(jnp.int32, (META, E), 0)
        meta = jnp.where(row == 0, first, jnp.where(row == 1, second, 0.0))
        out_ref[h, ROWS:PAY, :] = meta.astype(jnp.bfloat16)


def payload(*halves):
    vmem = pl.BlockSpec(memory_space=pltpu.VMEM)
    return pl.pallas_call(
        unit_kernel,
        out_shape=jax.ShapeDtypeStruct((2, PAY, E), jnp.bfloat16),
        in_specs=[vmem] * 6,
        out_specs=vmem,
        compiler_params=pltpu.CompilerParams(vmem_limit_bytes=GRANT),
        cost_estimate=pl.CostEstimate(flops=2000000, bytes_accessed=1600000, transcendentals=512),
    )(*halves)


def cube_code():
    group, tile = lax.axis_index("group"), lax.axis_index("tile")
    side = group & 1
    bits = [(place >> side) & 1 for place in (tile & 3, tile >> 2, group >> 1)]
    return bits[0] | (bits[1] << 1) | (bits[2] << 2)


def match_kernel(queries, keys, begin, *refs):
    mine = dict(zip(queries, refs[0 : len(queries)]))
    theirs = dict(zip(keys, refs[len(queries) : len(queries) + len(keys)]))
    out_ref, first, second = refs[-3:]

    def numbers(meta):
        meta = meta.astype(jnp.float32)
        rank = meta[0:1, 0:ROWS] * 256.0 + meta[0:1, ROWS : 2 * ROWS]
        return rank, meta[1:2, 0:ROWS] * 32768.0 + rank

    def columns(row):
        return jnp.broadcast_to(jnp.transpose(jnp.broadcast_to(row, (8, ROWS)))[:, 0:1], (ROWS, 128)).astype(jnp.int32)

    def product(left, right):
        return lax.dot_general(left, right, (((1,), (1,)), ((), ())), preferred_element_type=jnp.float32)

    found = {}
    sides = [(n, h) for n in keys for h in range(2)]
    limits = {m: numbers(mine[m][0, ROWS:PAY, :]) for m in queries}
    wanted = {(n, h): numbers(theirs[n][h, ROWS:PAY, :])[1] for n, h in sides}
    if len(queries) < len(keys):
        for i, m in enumerate(queries):
            first[i] = columns(limits[m][1])
            second[i] = columns(limits[m][0]) + LOW
        rows = {side: wanted[side].astype(jnp.int32) + (LOW + 1) for side in sides}
        for i, m in enumerate(queries):
            best = jnp.full((ROWS, 128), -1.0, jnp.float32)
            for n, h in sides:
                score = product(mine[m][0, 0:ROWS, :], theirs[n][h, 0:ROWS, :])
                for lanes in (slice(0, 128), slice(128, 256)):
                    valid = first[i] - rows[n, h][:, lanes] < second[i]
                    best = jnp.maximum(best, jnp.where(valid, score[:, lanes], -1.0))
            found[m] = jnp.max(jnp.transpose(best), axis=0, keepdims=True)
    else:
        for i, side in enumerate(sides):
            first[i] = columns(wanted[side]) + (LOW + 1)
        for m in queries:
            row = jnp.broadcast_to(limits[m][1].astype(jnp.int32), (8, ROWS))
            limit = jnp.broadcast_to(limits[m][0].astype(jnp.int32) + LOW, (8, ROWS))
            best = jnp.full((8, ROWS), -1.0, jnp.float32)
            for i, (n, h) in enumerate(sides):
                score = product(theirs[n][h, 0:ROWS, :], mine[m][0, 0:ROWS, :])
                for r in range(0, ROWS, 8):
                    column = first[i, r : r + 8, :]
                    valid = row - jnp.concatenate([column, column], axis=1) < limit
                    best = jnp.maximum(best, jnp.where(valid, score[r : r + 8, :], -1.0))
            found[m] = jnp.max(best, axis=0, keepdims=True)
    code = cube_code()
    out_ref[...] = jnp.full(out_ref.shape, -1.0, jnp.float32) if begin else refs[-4][...]
    for m in queries:
        slot = code ^ m
        out_ref[slot] = jnp.maximum(out_ref[slot], found[m])


def match(queries, keys, mine, theirs, *prev):
    columns = len(queries) if len(queries) < len(keys) else 2 * len(keys)
    vmem = pl.BlockSpec(memory_space=pltpu.VMEM)
    return pl.pallas_call(
        functools.partial(match_kernel, queries, keys, not prev),
        out_shape=jax.ShapeDtypeStruct((8, 1, ROWS), jnp.float32),
        in_specs=[vmem] * (len(queries) + len(keys) + len(prev)),
        out_specs=vmem,
        scratch_shapes=[pltpu.VMEM((columns, ROWS, 128), jnp.int32)] * 2,
        compiler_params=pltpu.CompilerParams(vmem_limit_bytes=GRANT),
        cost_estimate=pl.CostEstimate(
            flops=len(queries) * len(keys) * 2 * ROWS * 2 * ROWS * E, bytes_accessed=1000, transcendentals=0
        ),
    )(*[mine[m] for m in queries], *[theirs[m] for m in keys], *prev)


def on_device(embeddings, cluster_ids, order_rank):
    half = (embeddings, cluster_ids.reshape(1, ROWS), order_rank.reshape(1, ROWS))
    own = payload(*half, *[swap(part) for part in half])
    mine, theirs = {0: own}, {0: own}
    for m in (1, 2, 4):
        mine[m] = exchange(own, m)
    mine[3] = exchange(mine[1], 2)
    mine[6] = exchange(mine[2], 4)
    mine[5] = exchange(mine[4], 1)
    best = match((0, 1, 2, 4), (0,), mine, theirs)
    theirs.update({m: swap(mine[m]) for m in (1, 2, 4)})
    best = match((0, 1, 2, 4), (1, 2, 4), mine, theirs, best)
    mine[3], mine[6], mine[5], best = lax.optimization_barrier((mine[3], mine[6], mine[5], best))
    mine[7] = exchange(mine[3], 4)
    best = match((3, 6, 5), (0, 1, 2, 4), mine, theirs, best)
    theirs.update({m: swap(mine[m]) for m in (3, 6, 5)})
    best = match((0, 1, 2, 4, 3, 6, 5), (3, 6, 5), mine, theirs, best)
    mine[7], best = lax.optimization_barrier((mine[7], best))
    theirs[7] = swap(mine[7])
    best = match((7,), (0, 1, 2, 4, 3, 6, 5), mine, theirs, best)
    best = match((0, 1, 2, 4, 3, 6, 5, 7), (7,), mine, theirs, best)
    back = lax.all_to_all(best, AXES, split_axis=0, concat_axis=0, axis_index_groups=cube_groups())
    return jnp.max(back, axis=0)[0]


def solution(mesh):
    return jax.shard_map(
        on_device,
        mesh=mesh,
        in_specs=(P(AXES, None), P(AXES, None), P(AXES)),
        out_specs=P(AXES),
        check_vma=False,
    )
```

```python
import functools

import jax
import jax.numpy as jnp
from jax import lax
from jax.experimental import pallas as pl
from jax.experimental.pallas import tpu as pltpu
from jax.sharding import PartitionSpec as P

AXES = ("group", "tile")
ROWS = 256
META = 16
PAY = ROWS + META
E = 512
LOW = -(2**31)
GRANT = 12 * 2**20
SMALL = pl.CostEstimate(flops=1000, bytes_accessed=1000, transcendentals=0)
NEAR = (1, 0, 3, 2)
OTHER = (3, 2, 1, 0)
PLACES = [(x, y, z, c) for x in range(4) for y in range(4) for z in range(4) for c in range(2)]


def linear(x, y, z, c):
    return (z * 2 + c) * 16 + y * 4 + x


def across(place, mask):
    x, y, z, c = place
    step = OTHER if c else NEAR
    return (
        step[x] if mask & 1 else x,
        step[y] if mask & 2 else y,
        step[z] if mask & 4 else z,
        c,
    )


def exchange(array, mask):
    pairs = [(linear(*across(q, mask)), linear(*q)) for q in PLACES]
    return lax.ppermute(array, AXES, pairs)


def swap(array):
    pairs = [(linear(x, y, z, 1 - c), linear(x, y, z, c)) for x, y, z, c in PLACES]
    return lax.ppermute(array, AXES, pairs)


def cube_groups():
    groups = []
    for place in PLACES:
        starts = (0, 1) if place[3] else (0, 2)
        if all(p in starts for p in place[:3]):
            groups.append([linear(*across(place, k)) for k in range(8)])
    return groups


def unit_kernel(emb_hbm, cluster_hbm, rank_hbm, out_ref, emb_ref, cluster_ref, rank_ref, sem):
    sources = (cluster_hbm, rank_hbm, emb_hbm)
    targets = (cluster_ref, rank_ref, emb_ref)
    copies = [pltpu.make_async_copy(a, b, sem.at[i]) for i, (a, b) in enumerate(zip(sources, targets))]
    for copy in copies:
        copy.start()
    for copy in copies:
        copy.wait()
    emb = emb_ref[...]
    sums = jnp.sum(emb * emb, axis=1, keepdims=True)
    out_ref[0:ROWS, :] = (emb * lax.rsqrt(sums + 1e-06)).astype(jnp.bfloat16)
    rank = rank_ref[...]
    high = (rank >> 8).astype(jnp.float32)
    low = (rank & 255).astype(jnp.float32)
    cluster = cluster_ref[...].astype(jnp.float32)
    first = jnp.concatenate([high, low], axis=1)
    second = jnp.concatenate([cluster, jnp.zeros_like(cluster)], axis=1)
    row = lax.broadcasted_iota(jnp.int32, (META, E), 0)
    meta = jnp.where(row == 0, first, jnp.where(row == 1, second, 0.0))
    out_ref[ROWS:PAY, :] = meta.astype(jnp.bfloat16)


def payload(embeddings, cluster_ids, order_rank):
    anywhere = pl.BlockSpec(memory_space=pl.ANY)
    return pl.pallas_call(
        unit_kernel,
        out_shape=jax.ShapeDtypeStruct((PAY, E), jnp.bfloat16),
        in_specs=[anywhere] * 3,
        out_specs=pl.BlockSpec(memory_space=pltpu.VMEM),
        scratch_shapes=[
            pltpu.VMEM((ROWS, E), jnp.float32),
            pltpu.VMEM((1, ROWS), jnp.int32),
            pltpu.VMEM((1, ROWS), jnp.int32),
            pltpu.SemaphoreType.DMA((3,)),
        ],
        compiler_params=pltpu.CompilerParams(vmem_limit_bytes=GRANT),
        cost_estimate=SMALL,
    )(embeddings, cluster_ids.reshape(1, ROWS), order_rank.reshape(1, ROWS))


def join_kernel(first_ref, second_ref, out_ref):
    out_ref[0] = first_ref[...]
    out_ref[1] = second_ref[...]


def join(first, second):
    vmem = pl.BlockSpec(memory_space=pltpu.VMEM)
    return pl.pallas_call(
        join_kernel,
        out_shape=jax.ShapeDtypeStruct((2, PAY, E), jnp.bfloat16),
        in_specs=[vmem] * 2,
        out_specs=vmem,
        compiler_params=pltpu.CompilerParams(vmem_limit_bytes=GRANT),
        cost_estimate=SMALL,
    )(first, second)


def pack_kernel(*refs):
    half = len(refs) // 2
    for source, out in zip(refs[:half], refs[half:]):
        out[0:ROWS, :] = source[0, 0:ROWS, :]
        out[ROWS : 2 * ROWS, :] = source[1, 0:ROWS, :]
        one = source[0, ROWS:PAY, :].astype(jnp.float32)
        two = source[1, ROWS:PAY, :].astype(jnp.float32)
        both = jnp.concatenate([one[0:2], two[0:2], jnp.zeros((META - 4, E), jnp.float32)], axis=0)
        out[2 * ROWS : 2 * ROWS + META, :] = both.astype(jnp.bfloat16)


def pack(*blocks):
    vmem = pl.BlockSpec(memory_space=pltpu.VMEM)
    return pl.pallas_call(
        pack_kernel,
        out_shape=[jax.ShapeDtypeStruct((2 * ROWS + META, E), jnp.bfloat16)] * len(blocks),
        in_specs=[vmem] * len(blocks),
        out_specs=[vmem] * len(blocks),
        compiler_params=pltpu.CompilerParams(vmem_limit_bytes=GRANT),
        cost_estimate=SMALL,
    )(*blocks)


def cube_code():
    group, tile = lax.axis_index("group"), lax.axis_index("tile")
    side = group & 1
    bits = [(place >> side) & 1 for place in (tile & 3, tile >> 2, group >> 1)]
    return bits[0] | (bits[1] << 1) | (bits[2] << 2)


def match_kernel(queries, keys, masks, begin, *refs):
    mine = dict(zip(masks, refs[0 : len(masks)]))
    others = [n for n in keys if n]
    theirs = dict(zip(others, refs[len(masks) : len(masks) + len(others)]))
    out_ref, first, second = refs[-3:]

    def numbers(meta, at):
        rank = meta[at : at + 1, 0:ROWS] * 256.0 + meta[at : at + 1, ROWS : 2 * ROWS]
        return rank, meta[at + 1 : at + 2, 0:ROWS] * 32768.0 + rank

    def columns(row):
        return jnp.broadcast_to(jnp.transpose(jnp.broadcast_to(row, (8, ROWS)))[:, 0:1], (ROWS, 128)).astype(jnp.int32)

    def product(left, right):
        return lax.dot_general(left, right, (((1,), (1,)), ((), ())), preferred_element_type=jnp.float32)

    def ask(m):
        return mine[m][0, 0:ROWS, :]

    def give(n, h):
        return theirs[n][h * ROWS : h * ROWS + ROWS, :] if n else mine[0][h, 0:ROWS, :]

    def given(n, h):
        meta = theirs[n][2 * ROWS : 2 * ROWS + META, :] if n else mine[0][h, ROWS:PAY, :]
        return numbers(meta.astype(jnp.float32), 2 * h if n else 0)[1]

    found = {}
    sides = [(n, h) for n in keys for h in range(2)]
    limits = {m: numbers(mine[m][0, ROWS:PAY, :].astype(jnp.float32), 0) for m in queries}
    wanted = {side: given(*side) for side in sides}
    if len(queries) < len(keys):
        for i, m in enumerate(queries):
            first[i] = columns(limits[m][1])
            second[i] = columns(limits[m][0]) + LOW
        rows = {side: wanted[side].astype(jnp.int32) + (LOW + 1) for side in sides}
        for i, m in enumerate(queries):
            best = jnp.full((ROWS, 128), -1.0, jnp.float32)
            for side in sides:
                score = product(ask(m), give(*side))
                for lanes in (slice(0, 128), slice(128, 256)):
                    valid = first[i] - rows[side][:, lanes] < second[i]
                    best = jnp.maximum(best, jnp.where(valid, score[:, lanes], -1.0))
            found[m] = jnp.max(jnp.transpose(best), axis=0, keepdims=True)
    else:
        for i, side in enumerate(sides):
            first[i] = columns(wanted[side]) + (LOW + 1)
        for m in queries:
            row = jnp.broadcast_to(limits[m][1].astype(jnp.int32), (8, ROWS))
            limit = jnp.broadcast_to(limits[m][0].astype(jnp.int32) + LOW, (8, ROWS))
            best = jnp.full((8, ROWS), -1.0, jnp.float32)
            for i, side in enumerate(sides):
                score = product(give(*side), ask(m))
                for r in range(0, ROWS, 8):
                    column = first[i, r : r + 8, :]
                    valid = row - jnp.concatenate([column, column], axis=1) < limit
                    best = jnp.maximum(best, jnp.where(valid, score[r : r + 8, :], -1.0))
            found[m] = jnp.max(best, axis=0, keepdims=True)
    code = cube_code()
    out_ref[...] = jnp.full(out_ref.shape, -1.0, jnp.float32) if begin else refs[-4][...]
    for m in queries:
        slot = code ^ m
        out_ref[slot] = jnp.maximum(out_ref[slot], found[m])


def match(queries, keys, mine, theirs, *prev):
    masks = sorted(set(queries) | ({0} & set(keys)))
    others = [n for n in keys if n]
    columns = len(queries) if len(queries) < len(keys) else 2 * len(keys)
    vmem = pl.BlockSpec(memory_space=pltpu.VMEM)
    return pl.pallas_call(
        functools.partial(match_kernel, queries, keys, masks, not prev),
        out_shape=jax.ShapeDtypeStruct((8, 1, ROWS), jnp.float32),
        in_specs=[vmem] * (len(masks) + len(others) + len(prev)),
        out_specs=vmem,
        scratch_shapes=[pltpu.VMEM((columns, ROWS, 128), jnp.int32)] * 2,
        compiler_params=pltpu.CompilerParams(vmem_limit_bytes=GRANT),
        cost_estimate=SMALL,
    )(*[mine[m] for m in masks], *[theirs[n] for n in others], *prev)


def on_device(embeddings, cluster_ids, order_rank):
    unit = payload(embeddings, cluster_ids, order_rank)
    mine, theirs = {0: join(unit, swap(unit))}, {}
    near, far = (0, 1, 2, 4), (3, 6, 5)
    for m in (1, 2, 4):
        mine[m] = exchange(mine[0], m)
    mine[3] = exchange(mine[1], 2)
    mine[6] = exchange(mine[2], 4)
    mine[5] = exchange(mine[4], 1)
    theirs.update({m: swap(pack(mine[m])[0]) for m in (1, 2, 4)})
    best = match(near, near, mine, theirs)
    best, mine[3] = lax.optimization_barrier((best, mine[3]))
    mine[7] = exchange(mine[3], 4)
    theirs.update({m: swap(pack(mine[m])[0]) for m in far})
    best = match(far, near, mine, theirs, best)
    best = match((*near, *far), far, mine, theirs, best)
    best, mine[7] = lax.optimization_barrier((best, mine[7]))
    theirs[7] = swap(pack(mine[7])[0])
    best = match((7,), (*near, *far), mine, theirs, best)
    best = match((*near, *far, 7), (7,), mine, theirs, best)
    back = lax.all_to_all(best, AXES, split_axis=0, concat_axis=0, axis_index_groups=cube_groups())
    return jnp.max(back, axis=0)[0]


def solution(mesh):
    return jax.shard_map(
        on_device,
        mesh=mesh,
        in_specs=(P(AXES, None), P(AXES, None), P(AXES)),
        out_specs=P(AXES),
        check_vma=False,
    )
```

```python
import functools

import jax
import jax.numpy as jnp
from jax import lax
from jax.experimental import pallas as pl
from jax.experimental.pallas import tpu as pltpu
from jax.sharding import PartitionSpec as P

AXES = ("group", "tile")
ROWS = 256
META = 16
PAY = ROWS + META
E = 512
LOW = -(2**31)
GRANT = 12 * 2**20
SMALL = pl.CostEstimate(flops=1000, bytes_accessed=1000, transcendentals=0)
NEAR = (1, 0, 3, 2)
OTHER = (3, 2, 1, 0)
PLACES = [(x, y, z, c) for x in range(4) for y in range(4) for z in range(4) for c in range(2)]


def linear(x, y, z, c):
    return (z * 2 + c) * 16 + y * 4 + x


def across(place, mask):
    x, y, z, c = place
    step = OTHER if c else NEAR
    return (
        step[x] if mask & 1 else x,
        step[y] if mask & 2 else y,
        step[z] if mask & 4 else z,
        c,
    )


def exchange(array, mask):
    pairs = [(linear(*across(q, mask)), linear(*q)) for q in PLACES]
    return lax.ppermute(array, AXES, pairs)


def swap(array):
    pairs = [(linear(x, y, z, 1 - c), linear(x, y, z, c)) for x, y, z, c in PLACES]
    return lax.ppermute(array, AXES, pairs)


def unit_kernel(emb_hbm, cluster_hbm, rank_hbm, out_ref, emb_ref, cluster_ref, rank_ref, sem):
    sources = (cluster_hbm, rank_hbm, emb_hbm)
    targets = (cluster_ref, rank_ref, emb_ref)
    copies = [pltpu.make_async_copy(a, b, sem.at[i]) for i, (a, b) in enumerate(zip(sources, targets))]
    for copy in copies:
        copy.start()
    for copy in copies:
        copy.wait()
    emb = emb_ref[...]
    sums = jnp.sum(emb * emb, axis=1, keepdims=True)
    out_ref[0:ROWS, :] = (emb * lax.rsqrt(sums + 1e-06)).astype(jnp.bfloat16)
    rank = rank_ref[...]
    high = (rank >> 8).astype(jnp.float32)
    low = (rank & 255).astype(jnp.float32)
    cluster = cluster_ref[...].astype(jnp.float32)
    first = jnp.concatenate([high, low], axis=1)
    second = jnp.concatenate([cluster, jnp.zeros_like(cluster)], axis=1)
    row = lax.broadcasted_iota(jnp.int32, (META, E), 0)
    meta = jnp.where(row == 0, first, jnp.where(row == 1, second, 0.0))
    out_ref[ROWS:PAY, :] = meta.astype(jnp.bfloat16)


def payload(embeddings, cluster_ids, order_rank):
    outside = pl.BlockSpec(memory_space=pltpu.HBM)
    return pl.pallas_call(
        unit_kernel,
        out_shape=jax.ShapeDtypeStruct((PAY, E), jnp.bfloat16),
        in_specs=[outside] * 3,
        out_specs=pl.BlockSpec(memory_space=pltpu.VMEM),
        scratch_shapes=[
            pltpu.VMEM((ROWS, E), jnp.float32),
            pltpu.VMEM((1, ROWS), jnp.int32),
            pltpu.VMEM((1, ROWS), jnp.int32),
            pltpu.SemaphoreType.DMA((3,)),
        ],
        compiler_params=pltpu.CompilerParams(vmem_limit_bytes=GRANT),
        cost_estimate=SMALL,
    )(*[pltpu.with_memory_space_constraint(x, pltpu.HBM) for x in (embeddings, cluster_ids.reshape(1, ROWS), order_rank.reshape(1, ROWS))])


def join_kernel(first_ref, second_ref, out_ref):
    out_ref[0] = first_ref[...]
    out_ref[1] = second_ref[...]


def join(first, second):
    vmem = pl.BlockSpec(memory_space=pltpu.VMEM)
    return pl.pallas_call(
        join_kernel,
        out_shape=jax.ShapeDtypeStruct((2, PAY, E), jnp.bfloat16),
        in_specs=[vmem] * 2,
        out_specs=vmem,
        compiler_params=pltpu.CompilerParams(vmem_limit_bytes=GRANT),
        cost_estimate=SMALL,
    )(first, second)


def pack_kernel(*refs):
    half = len(refs) // 2
    for source, out in zip(refs[:half], refs[half:]):
        out[0:ROWS, :] = source[0, 0:ROWS, :]
        out[ROWS : 2 * ROWS, :] = source[1, 0:ROWS, :]
        one = source[0, ROWS:PAY, :].astype(jnp.float32)
        two = source[1, ROWS:PAY, :].astype(jnp.float32)
        both = jnp.concatenate([one[0:2], two[0:2], jnp.zeros((META - 4, E), jnp.float32)], axis=0)
        out[2 * ROWS : 2 * ROWS + META, :] = both.astype(jnp.bfloat16)


def pack(*blocks):
    vmem = pl.BlockSpec(memory_space=pltpu.VMEM)
    return pl.pallas_call(
        pack_kernel,
        out_shape=[jax.ShapeDtypeStruct((2 * ROWS + META, E), jnp.bfloat16)] * len(blocks),
        in_specs=[vmem] * len(blocks),
        out_specs=[vmem] * len(blocks),
        compiler_params=pltpu.CompilerParams(vmem_limit_bytes=GRANT),
        cost_estimate=SMALL,
    )(*blocks)


def match_kernel(queries, keys, masks, begin, last, *refs):
    mine = dict(zip(masks, refs[0 : len(masks)]))
    others = [n for n in keys if n]
    theirs = dict(zip(others, refs[len(masks) : len(masks) + len(others)]))
    out_ref, first, second = refs[-4 if last else -3], *refs[-2:]

    def numbers(meta, at):
        rank = meta[at : at + 1, 0:ROWS] * 256.0 + meta[at : at + 1, ROWS : 2 * ROWS]
        return rank, meta[at + 1 : at + 2, 0:ROWS] * 32768.0 + rank

    def columns(row):
        return jnp.broadcast_to(jnp.transpose(jnp.broadcast_to(row, (8, ROWS)))[:, 0:1], (ROWS, 128)).astype(jnp.int32)

    def product(left, right):
        return lax.dot_general(left, right, (((1,), (1,)), ((), ())), preferred_element_type=jnp.float32)

    def ask(m):
        return mine[m][0, 0:ROWS, :]

    def give(n, h):
        return theirs[n][h * ROWS : h * ROWS + ROWS, :] if n else mine[0][h, 0:ROWS, :]

    def given(n, h):
        meta = theirs[n][2 * ROWS : 2 * ROWS + META, :] if n else mine[0][h, ROWS:PAY, :]
        return numbers(meta.astype(jnp.float32), 2 * h if n else 0)[1]

    found = {}
    sides = [(n, h) for n in keys for h in range(2)]
    limits = {m: numbers(mine[m][0, ROWS:PAY, :].astype(jnp.float32), 0) for m in queries}
    wanted = {side: given(*side) for side in sides}
    if len(queries) < len(keys):
        for i, m in enumerate(queries):
            first[i] = columns(limits[m][1])
            second[i] = columns(limits[m][0]) + LOW
        rows = {side: wanted[side].astype(jnp.int32) + (LOW + 1) for side in sides}
        for i, m in enumerate(queries):
            best = jnp.full((ROWS, 128), -1.0, jnp.float32)
            for side in sides:
                score = product(ask(m), give(*side))
                for lanes in (slice(0, 128), slice(128, 256)):
                    valid = first[i] - rows[side][:, lanes] < second[i]
                    best = jnp.maximum(best, jnp.where(valid, score[:, lanes], -1.0))
            found[m] = jnp.max(jnp.transpose(best), axis=0, keepdims=True)
    else:
        for i, side in enumerate(sides):
            first[i] = columns(wanted[side]) + (LOW + 1)
        for m in queries:
            row = jnp.broadcast_to(limits[m][1].astype(jnp.int32), (8, ROWS))
            limit = jnp.broadcast_to(limits[m][0].astype(jnp.int32) + LOW, (8, ROWS))
            best = jnp.full((8, ROWS), -1.0, jnp.float32)
            for i, side in enumerate(sides):
                score = product(give(*side), ask(m))
                for r in range(0, ROWS, 8):
                    column = first[i, r : r + 8, :]
                    valid = row - jnp.concatenate([column, column], axis=1) < limit
                    best = jnp.maximum(best, jnp.where(valid, score[r : r + 8, :], -1.0))
            found[m] = jnp.max(best, axis=0, keepdims=True)
    old = None if begin else refs[-5 if last else -4]
    for m in range(8):
        best = jnp.full((1, ROWS), -1.0, jnp.float32) if begin else old[m]
        best = jnp.maximum(best, found[m]) if m in found else best
        out_ref[m] = best
        if last and m > 3:
            refs[-3][m - 4] = best


def match(queries, keys, mine, theirs, *prev, last=False):
    masks = sorted(set(queries) | ({0} & set(keys)))
    others = [n for n in keys if n]
    columns = len(queries) if len(queries) < len(keys) else 2 * len(keys)
    vmem = pl.BlockSpec(memory_space=pltpu.VMEM)
    found = pl.pallas_call(
        functools.partial(match_kernel, queries, keys, masks, not prev, last),
        out_shape=[jax.ShapeDtypeStruct((k, 1, ROWS), jnp.float32) for k in ((8, 4) if last else (8,))],
        in_specs=[vmem] * (len(masks) + len(others) + len(prev)),
        out_specs=[vmem] * (2 if last else 1),
        scratch_shapes=[pltpu.VMEM((columns, ROWS, 128), jnp.int32)] * 2,
        compiler_params=pltpu.CompilerParams(vmem_limit_bytes=GRANT),
        cost_estimate=SMALL,
    )(*[mine[m] for m in masks], *[theirs[n] for n in others], *prev)
    return found if last else found[0]


def fold_kernel(held_ref, come_ref, *outs):
    rows = come_ref.shape[0]
    total = jnp.maximum(held_ref[0:rows], come_ref[...])
    if len(outs) == 1:
        outs[0][...] = total[0]
    else:
        outs[0][...] = total
        outs[1][...] = total[rows // 2 :]


def fold(held, come):
    rows = come.shape[0]
    vmem = pl.BlockSpec(memory_space=pltpu.VMEM)
    shapes = [jax.ShapeDtypeStruct((k, 1, ROWS), jnp.float32) for k in (rows, rows // 2)]
    return pl.pallas_call(
        fold_kernel,
        out_shape=shapes if rows > 1 else [jax.ShapeDtypeStruct((1, ROWS), jnp.float32)],
        in_specs=[vmem] * 2,
        out_specs=[vmem] * (2 if rows > 1 else 1),
        compiler_params=pltpu.CompilerParams(vmem_limit_bytes=GRANT),
        cost_estimate=SMALL,
    )(held, come)


def on_device(embeddings, cluster_ids, order_rank):
    unit = payload(embeddings, cluster_ids, order_rank)
    mine, theirs = {0: join(unit, swap(unit))}, {}
    near, far = (0, 1, 2, 4), (3, 6, 5)
    for m in (1, 2, 4):
        mine[m] = exchange(mine[0], m)
    mine[3] = exchange(mine[1], 2)
    mine[6] = exchange(mine[2], 4)
    mine[5] = exchange(mine[4], 1)
    theirs.update({m: swap(pack(mine[m])[0]) for m in (1, 2, 4)})
    best = match(near, near, mine, theirs)
    best, mine[3] = lax.optimization_barrier((best, mine[3]))
    mine[7] = exchange(mine[3], 4)
    theirs.update({m: swap(pack(mine[m])[0]) for m in far})
    best = match(far, near, mine, theirs, best)
    best = match((4, 6, 5), far, mine, theirs, best)
    best, mine[7] = lax.optimization_barrier((best, mine[7]))
    theirs[7] = swap(pack(mine[7])[0])
    best = match((7,), (*near, *far), mine, theirs, best)
    best, send = match((4, 6, 5, 7), (7,), mine, theirs, best, last=True)
    held = match((0, 1, 2, 3), (3, 6, 5, 7), mine, theirs, best)
    for mask in (4, 2):
        held, send = fold(held, exchange(send, mask))
    return fold(held, exchange(send, 1))[0].reshape(ROWS)


def solution(mesh):
    return jax.shard_map(
        on_device,
        mesh=mesh,
        in_specs=(P(AXES, None), P(AXES, None), P(AXES)),
        out_specs=P(AXES),
        check_vma=False,
    )
```

```python
import functools

import jax
import jax.numpy as jnp
from jax import lax
from jax.experimental import pallas as pl
from jax.experimental.pallas import tpu as pltpu
from jax.sharding import PartitionSpec as P

AXES = ("group", "tile")
ROWS = 256
META = 16
PAY = ROWS + META
E = 512
LOW = -(2**31)
GRANT = 12 * 2**20
SMALL = pl.CostEstimate(flops=1000, bytes_accessed=1000, transcendentals=0)
NEAR = (1, 0, 3, 2)
OTHER = (3, 2, 1, 0)
PLACES = [(x, y, z, c) for x in range(4) for y in range(4) for z in range(4) for c in range(2)]


def linear(x, y, z, c):
    return (z * 2 + c) * 16 + y * 4 + x


def across(place, mask):
    x, y, z, c = place
    step = OTHER if c else NEAR
    return (
        step[x] if mask & 1 else x,
        step[y] if mask & 2 else y,
        step[z] if mask & 4 else z,
        c,
    )


def exchange(array, mask):
    pairs = [(linear(*across(q, mask)), linear(*q)) for q in PLACES]
    return lax.ppermute(array, AXES, pairs)


def swap(array):
    pairs = [(linear(x, y, z, 1 - c), linear(x, y, z, c)) for x, y, z, c in PLACES]
    return lax.ppermute(array, AXES, pairs)


def unit_kernel(emb_hbm, cluster_hbm, rank_hbm, out_ref, emb_ref, cluster_ref, rank_ref, sem):
    sources = (cluster_hbm, rank_hbm, emb_hbm)
    targets = (cluster_ref, rank_ref, emb_ref)
    copies = [pltpu.make_async_copy(a, b, sem.at[i]) for i, (a, b) in enumerate(zip(sources, targets))]
    for copy in copies:
        copy.start()
    for copy in copies:
        copy.wait()
    emb = emb_ref[...]
    sums = jnp.sum(emb * emb, axis=1, keepdims=True)
    out_ref[0:ROWS, :] = (emb * lax.rsqrt(sums + 1e-06)).astype(jnp.bfloat16)
    rank = rank_ref[...]
    high = (rank >> 8).astype(jnp.float32)
    low = (rank & 255).astype(jnp.float32)
    cluster = cluster_ref[...].astype(jnp.float32)
    first = jnp.concatenate([high, low], axis=1)
    second = jnp.concatenate([cluster, jnp.zeros_like(cluster)], axis=1)
    row = lax.broadcasted_iota(jnp.int32, (META, E), 0)
    meta = jnp.where(row == 0, first, jnp.where(row == 1, second, 0.0))
    out_ref[ROWS:PAY, :] = meta.astype(jnp.bfloat16)


def payload(embeddings, cluster_ids, order_rank):
    outside = pl.BlockSpec(memory_space=pltpu.HBM)
    return pl.pallas_call(
        unit_kernel,
        out_shape=jax.ShapeDtypeStruct((PAY, E), jnp.bfloat16),
        in_specs=[outside] * 3,
        out_specs=pl.BlockSpec(memory_space=pltpu.VMEM),
        scratch_shapes=[
            pltpu.VMEM((ROWS, E), jnp.float32),
            pltpu.VMEM((1, ROWS), jnp.int32),
            pltpu.VMEM((1, ROWS), jnp.int32),
            pltpu.SemaphoreType.DMA((3,)),
        ],
        compiler_params=pltpu.CompilerParams(vmem_limit_bytes=GRANT),
        cost_estimate=SMALL,
    )(*[pltpu.with_memory_space_constraint(x, pltpu.HBM) for x in (embeddings, cluster_ids.reshape(1, ROWS), order_rank.reshape(1, ROWS))])


def join_kernel(first_ref, second_ref, out_ref):
    out_ref[0] = first_ref[...]
    out_ref[1] = second_ref[...]


def join(first, second):
    vmem = pl.BlockSpec(memory_space=pltpu.VMEM)
    return pl.pallas_call(
        join_kernel,
        out_shape=jax.ShapeDtypeStruct((2, PAY, E), jnp.bfloat16),
        in_specs=[vmem] * 2,
        out_specs=vmem,
        compiler_params=pltpu.CompilerParams(vmem_limit_bytes=GRANT),
        cost_estimate=SMALL,
    )(first, second)


def pack_kernel(*refs):
    half = len(refs) // 2
    for source, out in zip(refs[:half], refs[half:]):
        out[0:ROWS, :] = source[0, 0:ROWS, :]
        out[ROWS : 2 * ROWS, :] = source[1, 0:ROWS, :]
        one = source[0, ROWS:PAY, :].astype(jnp.float32)
        two = source[1, ROWS:PAY, :].astype(jnp.float32)
        both = jnp.concatenate([one[0:2], two[0:2], jnp.zeros((META - 4, E), jnp.float32)], axis=0)
        out[2 * ROWS : 2 * ROWS + META, :] = both.astype(jnp.bfloat16)


def pack(*blocks):
    vmem = pl.BlockSpec(memory_space=pltpu.VMEM)
    return pl.pallas_call(
        pack_kernel,
        out_shape=[jax.ShapeDtypeStruct((2 * ROWS + META, E), jnp.bfloat16)] * len(blocks),
        in_specs=[vmem] * len(blocks),
        out_specs=[vmem] * len(blocks),
        compiler_params=pltpu.CompilerParams(vmem_limit_bytes=GRANT),
        cost_estimate=SMALL,
    )(*blocks)


def match_kernel(queries, keys, masks, begin, last, *refs):
    mine = dict(zip(masks, refs[0 : len(masks)]))
    others = [n for n in keys if n]
    theirs = dict(zip(others, refs[len(masks) : len(masks) + len(others)]))
    out_ref, first, second = refs[-4 if last else -3], *refs[-2:]

    def numbers(meta, at):
        rank = meta[at : at + 1, 0:ROWS] * 256.0 + meta[at : at + 1, ROWS : 2 * ROWS]
        return rank, meta[at + 1 : at + 2, 0:ROWS] * 32768.0 + rank

    def columns(row):
        return jnp.broadcast_to(jnp.transpose(jnp.broadcast_to(row, (8, ROWS)))[:, 0:1], (ROWS, 128)).astype(jnp.int32)

    def product(left, right):
        return lax.dot_general(left, right, (((1,), (1,)), ((), ())), preferred_element_type=jnp.float32)

    def ask(m):
        return mine[m][0, 0:ROWS, :]

    def give(n, h):
        return theirs[n][h * ROWS : h * ROWS + ROWS, :] if n else mine[0][h, 0:ROWS, :]

    def given(n, h):
        meta = theirs[n][2 * ROWS : 2 * ROWS + META, :] if n else mine[0][h, ROWS:PAY, :]
        return numbers(meta.astype(jnp.float32), 2 * h if n else 0)[1]

    found = {}
    sides = [(n, h) for n in keys for h in range(2)]
    limits = {m: numbers(mine[m][0, ROWS:PAY, :].astype(jnp.float32), 0) for m in queries}
    wanted = {side: given(*side) for side in sides}
    if len(queries) < len(keys):
        for i, m in enumerate(queries):
            first[i] = columns(limits[m][1])
            second[i] = columns(limits[m][0]) + LOW
        rows = {side: wanted[side].astype(jnp.int32) + (LOW + 1) for side in sides}
        for i, m in enumerate(queries):
            best = jnp.full((ROWS, 128), -1.0, jnp.float32)
            for side in sides:
                score = product(ask(m), give(*side))
                for lanes in (slice(0, 128), slice(128, 256)):
                    valid = first[i] - rows[side][:, lanes] < second[i]
                    best = jnp.maximum(best, jnp.where(valid, score[:, lanes], -1.0))
            found[m] = jnp.max(jnp.transpose(best), axis=0, keepdims=True)
    else:
        for i, side in enumerate(sides):
            first[i] = columns(wanted[side]) + (LOW + 1)
        for m in queries:
            row = jnp.broadcast_to(limits[m][1].astype(jnp.int32), (8, ROWS))
            limit = jnp.broadcast_to(limits[m][0].astype(jnp.int32) + LOW, (8, ROWS))
            best = jnp.full((8, ROWS), -1.0, jnp.float32)
            for i, side in enumerate(sides):
                score = product(give(*side), ask(m))
                for r in range(0, ROWS, 8):
                    column = first[i, r : r + 8, :]
                    valid = row - jnp.concatenate([column, column], axis=1) < limit
                    best = jnp.maximum(best, jnp.where(valid, score[r : r + 8, :], -1.0))
            found[m] = jnp.max(best, axis=0, keepdims=True)
    old = None if begin else refs[-5 if last else -4]
    for m in range(8):
        best = jnp.full((1, ROWS), -1.0, jnp.float32) if begin else old[m]
        best = jnp.maximum(best, found[m]) if m in found else best
        out_ref[m] = best
        if last and m > 3:
            refs[-3][m - 4] = best


def match(queries, keys, mine, theirs, *prev, last=False):
    masks = sorted(set(queries) | ({0} & set(keys)))
    others = [n for n in keys if n]
    columns = len(queries) if len(queries) < len(keys) else 2 * len(keys)
    vmem = pl.BlockSpec(memory_space=pltpu.VMEM)
    found = pl.pallas_call(
        functools.partial(match_kernel, queries, keys, masks, not prev, last),
        out_shape=[jax.ShapeDtypeStruct((k, 1, ROWS), jnp.float32) for k in ((8, 4) if last else (8,))],
        in_specs=[vmem] * (len(masks) + len(others) + len(prev)),
        out_specs=[vmem] * (2 if last else 1),
        scratch_shapes=[pltpu.VMEM((columns, ROWS, 128), jnp.int32)] * 2,
        compiler_params=pltpu.CompilerParams(vmem_limit_bytes=GRANT),
        cost_estimate=SMALL,
    )(*[mine[m] for m in masks], *[theirs[n] for n in others], *prev)
    return found if last else found[0]


def fold_kernel(row, *refs):
    out_ref = refs[-1]
    total = refs[0][row : row + 1] if row < 2 else refs[0][row : row + 2]
    for come_ref in refs[1:-1]:
        total = jnp.maximum(total, come_ref[row : row + total.shape[0]])
    out_ref[...] = total if row else total[0]


def fold(row, *parts):
    vmem = pl.BlockSpec(memory_space=pltpu.VMEM)
    shape = {0: (1, ROWS), 1: (1, 1, ROWS), 2: (2, 1, ROWS)}[row]
    return pl.pallas_call(
        functools.partial(fold_kernel, row),
        out_shape=jax.ShapeDtypeStruct(shape, jnp.float32),
        in_specs=[vmem] * len(parts),
        out_specs=vmem,
        compiler_params=pltpu.CompilerParams(vmem_limit_bytes=GRANT),
        cost_estimate=SMALL,
    )(*parts)


def on_device(embeddings, cluster_ids, order_rank):
    unit = payload(embeddings, cluster_ids, order_rank)
    mine, theirs = {0: join(unit, swap(unit))}, {}
    near, far = (0, 1, 2, 4), (3, 6, 5)
    for m in (1, 2, 4):
        mine[m] = exchange(mine[0], m)
    mine[3] = exchange(mine[1], 2)
    mine[6] = exchange(mine[2], 4)
    mine[5] = exchange(mine[4], 1)
    theirs.update({m: swap(pack(mine[m])[0]) for m in (1, 2, 4)})
    mine[7] = exchange(mine[3], 4)
    theirs.update({m: swap(pack(mine[m])[0]) for m in far})
    every = (*near, *far, 7)
    best = match((4, 6, 5), near, mine, theirs)
    best = match((4, 6, 5), far, mine, theirs, best)
    best, mine[7] = lax.optimization_barrier((best, mine[7]))
    theirs[7] = swap(pack(mine[7])[0])
    best = match((7,), (*near, *far), mine, theirs, best)
    best, send = match((4, 6, 5, 7), (7,), mine, theirs, best, last=True)
    send, mine[0] = lax.optimization_barrier((send, mine[0]))
    first = exchange(send, 4)
    send = fold(2, match((2, 3), every, mine, theirs), first)
    send, mine[0] = lax.optimization_barrier((send, mine[0]))
    second = exchange(send, 2)
    send = fold(1, match((1,), every, mine, theirs), first, second)
    send, mine[0] = lax.optimization_barrier((send, mine[0]))
    third = exchange(send, 1)
    return fold(0, match((0,), every, mine, theirs), first, second, third).reshape(ROWS)


def solution(mesh):
    return jax.shard_map(
        on_device,
        mesh=mesh,
        in_specs=(P(AXES, None), P(AXES, None), P(AXES)),
        out_specs=P(AXES),
        check_vma=False,
    )
```

```python
import functools

import jax
import jax.numpy as jnp
from jax import lax
from jax.experimental import pallas as pl
from jax.experimental.pallas import tpu as pltpu
from jax.sharding import PartitionSpec as P

AXES = ("group", "tile")
ROWS = 256
META = 16
PAY = ROWS + META
E = 512
LOW = -(2**31)
GRANT = 12 * 2**20
SMALL = pl.CostEstimate(flops=1000, bytes_accessed=1000, transcendentals=0)
NEAR = (1, 0, 3, 2)
OTHER = (3, 2, 1, 0)
PLACES = [(x, y, z, c) for x in range(4) for y in range(4) for z in range(4) for c in range(2)]


def linear(x, y, z, c):
    return (z * 2 + c) * 16 + y * 4 + x


def across(place, mask):
    x, y, z, c = place
    step = OTHER if c else NEAR
    return (
        step[x] if mask & 1 else x,
        step[y] if mask & 2 else y,
        step[z] if mask & 4 else z,
        c,
    )


def exchange(array, mask):
    pairs = [(linear(*across(q, mask)), linear(*q)) for q in PLACES]
    return lax.ppermute(array, AXES, pairs)


def swap(array):
    pairs = [(linear(x, y, z, 1 - c), linear(x, y, z, c)) for x, y, z, c in PLACES]
    return lax.ppermute(array, AXES, pairs)


def unit_kernel(emb_hbm, cluster_hbm, rank_hbm, out_ref, emb_ref, cluster_ref, rank_ref, sem):
    sources = (cluster_hbm, rank_hbm, emb_hbm)
    targets = (cluster_ref, rank_ref, emb_ref)
    copies = [pltpu.make_async_copy(a, b, sem.at[i]) for i, (a, b) in enumerate(zip(sources, targets))]
    for copy in copies:
        copy.start()
    for copy in copies:
        copy.wait()
    emb = emb_ref[...]
    sums = jnp.sum(emb * emb, axis=1, keepdims=True)
    out_ref[0:ROWS, :] = (emb * lax.rsqrt(sums + 1e-06)).astype(jnp.bfloat16)
    rank = rank_ref[...]
    high = (rank >> 8).astype(jnp.float32)
    low = (rank & 255).astype(jnp.float32)
    cluster = cluster_ref[...].astype(jnp.float32)
    first = jnp.concatenate([high, low], axis=1)
    second = jnp.concatenate([cluster, jnp.zeros_like(cluster)], axis=1)
    row = lax.broadcasted_iota(jnp.int32, (META, E), 0)
    meta = jnp.where(row == 0, first, jnp.where(row == 1, second, 0.0))
    out_ref[ROWS:PAY, :] = meta.astype(jnp.bfloat16)


def payload(embeddings, cluster_ids, order_rank):
    outside = pl.BlockSpec(memory_space=pltpu.HBM)
    return pl.pallas_call(
        unit_kernel,
        out_shape=jax.ShapeDtypeStruct((PAY, E), jnp.bfloat16),
        in_specs=[outside] * 3,
        out_specs=pl.BlockSpec(memory_space=pltpu.VMEM),
        scratch_shapes=[
            pltpu.VMEM((ROWS, E), jnp.float32),
            pltpu.VMEM((1, ROWS), jnp.int32),
            pltpu.VMEM((1, ROWS), jnp.int32),
            pltpu.SemaphoreType.DMA((3,)),
        ],
        compiler_params=pltpu.CompilerParams(vmem_limit_bytes=GRANT),
        cost_estimate=SMALL,
    )(*[pltpu.with_memory_space_constraint(x, pltpu.HBM) for x in (embeddings, cluster_ids.reshape(1, ROWS), order_rank.reshape(1, ROWS))])


def join_kernel(first_ref, second_ref, out_ref):
    out_ref[0] = first_ref[...]
    out_ref[1] = second_ref[...]


def join(first, second):
    vmem = pl.BlockSpec(memory_space=pltpu.VMEM)
    return pl.pallas_call(
        join_kernel,
        out_shape=jax.ShapeDtypeStruct((2, PAY, E), jnp.bfloat16),
        in_specs=[vmem] * 2,
        out_specs=vmem,
        compiler_params=pltpu.CompilerParams(vmem_limit_bytes=GRANT),
        cost_estimate=SMALL,
    )(first, second)


def pack_kernel(*refs):
    half = len(refs) // 2
    for source, out in zip(refs[:half], refs[half:]):
        out[0:ROWS, :] = source[0, 0:ROWS, :]
        out[ROWS : 2 * ROWS, :] = source[1, 0:ROWS, :]
        one = source[0, ROWS:PAY, :].astype(jnp.float32)
        two = source[1, ROWS:PAY, :].astype(jnp.float32)
        both = jnp.concatenate([one[0:2], two[0:2], jnp.zeros((META - 4, E), jnp.float32)], axis=0)
        out[2 * ROWS : 2 * ROWS + META, :] = both.astype(jnp.bfloat16)


def pack(*blocks):
    vmem = pl.BlockSpec(memory_space=pltpu.VMEM)
    return pl.pallas_call(
        pack_kernel,
        out_shape=[jax.ShapeDtypeStruct((2 * ROWS + META, E), jnp.bfloat16)] * len(blocks),
        in_specs=[vmem] * len(blocks),
        out_specs=[vmem] * len(blocks),
        compiler_params=pltpu.CompilerParams(vmem_limit_bytes=GRANT),
        cost_estimate=SMALL,
    )(*blocks)


def match_kernel(queries, keys, masks, begin, last, *refs):
    mine = dict(zip(masks, refs[0 : len(masks)]))
    others = [n for n in keys if n]
    theirs = dict(zip(others, refs[len(masks) : len(masks) + len(others)]))
    out_ref, first, second = refs[-3:]

    def numbers(meta, at):
        rank = meta[at : at + 1, 0:ROWS] * 256.0 + meta[at : at + 1, ROWS : 2 * ROWS]
        return rank, meta[at + 1 : at + 2, 0:ROWS] * 32768.0 + rank

    def columns(row):
        return jnp.broadcast_to(jnp.transpose(jnp.broadcast_to(row, (8, ROWS)))[:, 0:1], (ROWS, 128)).astype(jnp.int32)

    def product(left, right):
        return lax.dot_general(left, right, (((1,), (1,)), ((), ())), preferred_element_type=jnp.float32)

    def ask(m):
        return mine[m][0, 0:ROWS, :]

    def give(n, h):
        return theirs[n][h * ROWS : h * ROWS + ROWS, :] if n else mine[0][h, 0:ROWS, :]

    def given(n, h):
        meta = theirs[n][2 * ROWS : 2 * ROWS + META, :] if n else mine[0][h, ROWS:PAY, :]
        return numbers(meta.astype(jnp.float32), 2 * h if n else 0)[1]

    found = {}
    sides = [(n, h) for n in keys for h in range(2)]
    limits = {m: numbers(mine[m][0, ROWS:PAY, :].astype(jnp.float32), 0) for m in queries}
    wanted = {side: given(*side) for side in sides}
    if len(queries) < len(keys):
        for i, m in enumerate(queries):
            first[i] = columns(limits[m][1])
            second[i] = columns(limits[m][0]) + LOW
        rows = {side: wanted[side].astype(jnp.int32) + (LOW + 1) for side in sides}
        for i, m in enumerate(queries):
            best = jnp.full((ROWS, 128), -1.0, jnp.float32)
            for side in sides:
                score = product(ask(m), give(*side))
                for lanes in (slice(0, 128), slice(128, 256)):
                    valid = first[i] - rows[side][:, lanes] < second[i]
                    best = jnp.maximum(best, jnp.where(valid, score[:, lanes], -1.0))
            found[m] = jnp.max(jnp.transpose(best), axis=0, keepdims=True)
    else:
        for i, side in enumerate(sides):
            first[i] = columns(wanted[side]) + (LOW + 1)
        for m in queries:
            row = jnp.broadcast_to(limits[m][1].astype(jnp.int32), (8, ROWS))
            limit = jnp.broadcast_to(limits[m][0].astype(jnp.int32) + LOW, (8, ROWS))
            best = jnp.full((8, ROWS), -1.0, jnp.float32)
            for i, side in enumerate(sides):
                score = product(give(*side), ask(m))
                for r in range(0, ROWS, 8):
                    column = first[i, r : r + 8, :]
                    valid = row - jnp.concatenate([column, column], axis=1) < limit
                    best = jnp.maximum(best, jnp.where(valid, score[r : r + 8, :], -1.0))
            found[m] = jnp.max(best, axis=0, keepdims=True)
    old = None if begin else refs[-4]
    skip = 4 if last else 0
    for m in range(skip, 8):
        best = jnp.full((1, ROWS), -1.0, jnp.float32) if begin else old[m]
        best = jnp.maximum(best, found[m]) if m in found else best
        out_ref[m - skip] = best


def match(queries, keys, mine, theirs, *prev, last=False):
    masks = sorted(set(queries) | ({0} & set(keys)))
    others = [n for n in keys if n]
    columns = len(queries) if len(queries) < len(keys) else 2 * len(keys)
    vmem = pl.BlockSpec(memory_space=pltpu.VMEM)
    return pl.pallas_call(
        functools.partial(match_kernel, queries, keys, masks, not prev, last),
        out_shape=jax.ShapeDtypeStruct((4 if last else 8, 1, ROWS), jnp.float32),
        in_specs=[vmem] * (len(masks) + len(others) + len(prev)),
        out_specs=vmem,
        scratch_shapes=[pltpu.VMEM((columns, ROWS, 128), jnp.int32)] * 2,
        compiler_params=pltpu.CompilerParams(vmem_limit_bytes=GRANT),
        cost_estimate=SMALL,
    )(*[mine[m] for m in masks], *[theirs[n] for n in others], *prev)


def fold_kernel(row, *refs):
    out_ref = refs[-1]
    total = refs[0][row : row + 1] if row < 2 else refs[0][row : row + 2]
    for come_ref in refs[1:-1]:
        total = jnp.maximum(total, come_ref[row : row + total.shape[0]])
    out_ref[...] = total if row else total[0]


def fold(row, *parts):
    vmem = pl.BlockSpec(memory_space=pltpu.VMEM)
    shape = {0: (1, ROWS), 1: (1, 1, ROWS), 2: (2, 1, ROWS)}[row]
    return pl.pallas_call(
        functools.partial(fold_kernel, row),
        out_shape=jax.ShapeDtypeStruct(shape, jnp.float32),
        in_specs=[vmem] * len(parts),
        out_specs=vmem,
        compiler_params=pltpu.CompilerParams(vmem_limit_bytes=GRANT),
        cost_estimate=SMALL,
    )(*parts)


def on_device(embeddings, cluster_ids, order_rank):
    unit = payload(embeddings, cluster_ids, order_rank)
    mine, theirs = {0: join(unit, swap(unit))}, {}
    near, far = (0, 1, 2, 4), (3, 6, 5)
    for m in (1, 2, 4):
        mine[m] = exchange(mine[0], m)
    mine[3] = exchange(mine[1], 2)
    mine[6] = exchange(mine[2], 4)
    mine[5] = exchange(mine[4], 1)
    theirs.update({m: swap(pack(mine[m])[0]) for m in (1, 2, 4)})
    mine[7] = exchange(mine[3], 4)
    theirs.update({m: swap(pack(mine[m])[0]) for m in far})
    every = (*near, *far, 7)
    best = match((4, 6, 5), near, mine, theirs)
    best = match((4, 6, 5), far, mine, theirs, best)
    best, mine[7] = lax.optimization_barrier((best, mine[7]))
    theirs[7] = swap(pack(mine[7])[0])
    best = match((7,), (*near, *far), mine, theirs, best)
    send = match((4, 6, 5, 7), (7,), mine, theirs, best, last=True)
    send, mine[0] = lax.optimization_barrier((send, mine[0]))
    first = exchange(send, 4)
    send = fold(2, match((2, 3), every, mine, theirs), first)
    send, mine[0] = lax.optimization_barrier((send, mine[0]))
    second = exchange(send, 2)
    send = fold(1, match((1,), every, mine, theirs), first, second)
    send, mine[0] = lax.optimization_barrier((send, mine[0]))
    third = exchange(send, 1)
    return fold(0, match((0,), every, mine, theirs), first, second, third).reshape(ROWS)


def solution(mesh):
    return jax.shard_map(
        on_device,
        mesh=mesh,
        in_specs=(P(AXES, None), P(AXES, None), P(AXES)),
        out_specs=P(AXES),
        check_vma=False,
    )
```

```python
import functools

import jax
import jax.numpy as jnp
from jax import lax
from jax.experimental import pallas as pl
from jax.experimental.pallas import tpu as pltpu
from jax.sharding import PartitionSpec as P

AXES = ("group", "tile")
ROWS = 256
META = 16
PAY = ROWS + META
E = 512
LOW = -(2**31)
GRANT = 12 * 2**20
SMALL = pl.CostEstimate(flops=1000, bytes_accessed=1000, transcendentals=0)
NEAR = (1, 0, 3, 2)
OTHER = (3, 2, 1, 0)
PLACES = [(x, y, z, c) for x in range(4) for y in range(4) for z in range(4) for c in range(2)]


def linear(x, y, z, c):
    return (z * 2 + c) * 16 + y * 4 + x


def across(place, mask):
    x, y, z, c = place
    step = OTHER if c else NEAR
    return (
        step[x] if mask & 1 else x,
        step[y] if mask & 2 else y,
        step[z] if mask & 4 else z,
        c,
    )


def exchange(array, mask):
    pairs = [(linear(*across(q, mask)), linear(*q)) for q in PLACES]
    return lax.ppermute(array, AXES, pairs)


def swap(array):
    pairs = [(linear(x, y, z, 1 - c), linear(x, y, z, c)) for x, y, z, c in PLACES]
    return lax.ppermute(array, AXES, pairs)


def unit_kernel(emb_hbm, cluster_hbm, rank_hbm, out_ref, emb_ref, cluster_ref, rank_ref, sem):
    sources = (cluster_hbm, rank_hbm, emb_hbm)
    targets = (cluster_ref, rank_ref, emb_ref)
    copies = [pltpu.make_async_copy(a, b, sem.at[i]) for i, (a, b) in enumerate(zip(sources, targets))]
    for copy in copies:
        copy.start()
    for copy in copies:
        copy.wait()
    emb = emb_ref[...]
    sums = jnp.sum(emb * emb, axis=1, keepdims=True)
    out_ref[0:ROWS, :] = (emb * lax.rsqrt(sums + 1e-06)).astype(jnp.bfloat16)
    rank = rank_ref[...]
    high = (rank >> 8).astype(jnp.float32)
    low = (rank & 255).astype(jnp.float32)
    cluster = cluster_ref[...].astype(jnp.float32)
    first = jnp.concatenate([high, low], axis=1)
    second = jnp.concatenate([cluster, jnp.zeros_like(cluster)], axis=1)
    row = lax.broadcasted_iota(jnp.int32, (META, E), 0)
    meta = jnp.where(row == 0, first, jnp.where(row == 1, second, 0.0))
    out_ref[ROWS:PAY, :] = meta.astype(jnp.bfloat16)


def payload(embeddings, cluster_ids, order_rank):
    outside = pl.BlockSpec(memory_space=pltpu.HBM)
    return pl.pallas_call(
        unit_kernel,
        out_shape=jax.ShapeDtypeStruct((PAY, E), jnp.bfloat16),
        in_specs=[outside] * 3,
        out_specs=pl.BlockSpec(memory_space=pltpu.VMEM),
        scratch_shapes=[
            pltpu.VMEM((ROWS, E), jnp.float32),
            pltpu.VMEM((1, ROWS), jnp.int32),
            pltpu.VMEM((1, ROWS), jnp.int32),
            pltpu.SemaphoreType.DMA((3,)),
        ],
        compiler_params=pltpu.CompilerParams(vmem_limit_bytes=GRANT),
        cost_estimate=SMALL,
    )(*[pltpu.with_memory_space_constraint(x, pltpu.HBM) for x in (embeddings, cluster_ids.reshape(1, ROWS), order_rank.reshape(1, ROWS))])


def join_kernel(first_ref, second_ref, out_ref):
    out_ref[0] = first_ref[...]
    out_ref[1] = second_ref[...]


def join(first, second):
    vmem = pl.BlockSpec(memory_space=pltpu.VMEM)
    return pl.pallas_call(
        join_kernel,
        out_shape=jax.ShapeDtypeStruct((2, PAY, E), jnp.bfloat16),
        in_specs=[vmem] * 2,
        out_specs=vmem,
        compiler_params=pltpu.CompilerParams(vmem_limit_bytes=GRANT),
        cost_estimate=SMALL,
    )(first, second)


def pack_kernel(*refs):
    half = len(refs) // 2
    for source, out in zip(refs[:half], refs[half:]):
        out[0:ROWS, :] = source[0, 0:ROWS, :]
        out[ROWS : 2 * ROWS, :] = source[1, 0:ROWS, :]
        one = source[0, ROWS:PAY, :].astype(jnp.float32)
        two = source[1, ROWS:PAY, :].astype(jnp.float32)
        both = jnp.concatenate([one[0:2], two[0:2], jnp.zeros((META - 4, E), jnp.float32)], axis=0)
        out[2 * ROWS : 2 * ROWS + META, :] = both.astype(jnp.bfloat16)


def pack(*blocks):
    vmem = pl.BlockSpec(memory_space=pltpu.VMEM)
    return pl.pallas_call(
        pack_kernel,
        out_shape=[jax.ShapeDtypeStruct((2 * ROWS + META, E), jnp.bfloat16)] * len(blocks),
        in_specs=[vmem] * len(blocks),
        out_specs=[vmem] * len(blocks),
        compiler_params=pltpu.CompilerParams(vmem_limit_bytes=GRANT),
        cost_estimate=SMALL,
    )(*blocks)


def match_kernel(queries, keys, masks, begin, last, *refs):
    mine = dict(zip(masks, refs[0 : len(masks)]))
    others = [n for n in keys if n]
    theirs = dict(zip(others, refs[len(masks) : len(masks) + len(others)]))
    out_ref, first, second = refs[-3:]

    def numbers(meta, at):
        rank = meta[at : at + 1, 0:ROWS] * 256.0 + meta[at : at + 1, ROWS : 2 * ROWS]
        return rank, meta[at + 1 : at + 2, 0:ROWS] * 32768.0 + rank

    def columns(row):
        return jnp.broadcast_to(jnp.transpose(jnp.broadcast_to(row, (8, ROWS)))[:, 0:1], (ROWS, 128)).astype(jnp.int32)

    def product(left, right):
        return lax.dot_general(left, right, (((1,), (1,)), ((), ())), preferred_element_type=jnp.float32)

    def ask(m):
        return mine[m][0, 0:ROWS, :]

    def give(n, h):
        return theirs[n][h * ROWS : h * ROWS + ROWS, :] if n else mine[0][h, 0:ROWS, :]

    def given(n, h):
        meta = theirs[n][2 * ROWS : 2 * ROWS + META, :] if n else mine[0][h, ROWS:PAY, :]
        return numbers(meta.astype(jnp.float32), 2 * h if n else 0)[1]

    found = {}
    sides = [(n, h) for n in keys for h in range(2)]
    limits = {m: numbers(mine[m][0, ROWS:PAY, :].astype(jnp.float32), 0) for m in queries}
    wanted = {side: given(*side) for side in sides}
    if len(queries) < len(keys):
        for i, m in enumerate(queries):
            first[i] = columns(limits[m][1])
            second[i] = columns(limits[m][0]) + LOW
        rows = {side: wanted[side].astype(jnp.int32) + (LOW + 1) for side in sides}
        for i, m in enumerate(queries):
            best = jnp.full((ROWS, 128), -1.0, jnp.float32)
            for side in sides:
                score = product(ask(m), give(*side))
                for lanes in (slice(0, 128), slice(128, 256)):
                    valid = first[i] - rows[side][:, lanes] < second[i]
                    best = jnp.maximum(best, jnp.where(valid, score[:, lanes], -1.0))
            found[m] = jnp.max(jnp.transpose(best), axis=0, keepdims=True)
    else:
        for i, side in enumerate(sides):
            first[i] = columns(wanted[side]) + (LOW + 1)
        for m in queries:
            row = jnp.broadcast_to(limits[m][1].astype(jnp.int32), (8, ROWS))
            limit = jnp.broadcast_to(limits[m][0].astype(jnp.int32) + LOW, (8, ROWS))
            best = jnp.full((8, ROWS), -1.0, jnp.float32)
            for i, side in enumerate(sides):
                score = product(give(*side), ask(m))
                for r in range(0, ROWS, 8):
                    column = first[i, r : r + 8, :]
                    valid = row - jnp.concatenate([column, column], axis=1) < limit
                    best = jnp.maximum(best, jnp.where(valid, score[r : r + 8, :], -1.0))
            found[m] = jnp.max(best, axis=0, keepdims=True)
    old = None if begin else refs[-4]
    skip = 4 if last else 0
    for m in range(skip, 8):
        best = jnp.full((1, ROWS), -1.0, jnp.float32) if begin else old[m]
        best = jnp.maximum(best, found[m]) if m in found else best
        out_ref[m - skip] = best


def match(queries, keys, mine, theirs, *prev, last=False):
    masks = sorted(set(queries) | ({0} & set(keys)))
    others = [n for n in keys if n]
    columns = len(queries) if len(queries) < len(keys) else 2 * len(keys)
    vmem = pl.BlockSpec(memory_space=pltpu.VMEM)
    return pl.pallas_call(
        functools.partial(match_kernel, queries, keys, masks, not prev, last),
        out_shape=jax.ShapeDtypeStruct((4 if last else 8, 1, ROWS), jnp.float32),
        in_specs=[vmem] * (len(masks) + len(others) + len(prev)),
        out_specs=vmem,
        scratch_shapes=[pltpu.VMEM((columns, ROWS, 128), jnp.int32)] * 2,
        compiler_params=pltpu.CompilerParams(vmem_limit_bytes=GRANT),
        cost_estimate=SMALL,
    )(*[mine[m] for m in masks], *[theirs[n] for n in others], *prev)


def fold_kernel(row, *refs):
    out_ref = refs[-1]
    total = refs[0][row : row + 1] if row < 2 else refs[0][row : row + 2]
    for come_ref in refs[1:-1]:
        total = jnp.maximum(total, come_ref[row : row + total.shape[0]])
    out_ref[...] = total if row else total[0]


def fold(row, *parts):
    vmem = pl.BlockSpec(memory_space=pltpu.VMEM)
    shape = {0: (1, ROWS), 1: (1, 1, ROWS), 2: (2, 1, ROWS)}[row]
    return pl.pallas_call(
        functools.partial(fold_kernel, row),
        out_shape=jax.ShapeDtypeStruct(shape, jnp.float32),
        in_specs=[vmem] * len(parts),
        out_specs=vmem,
        compiler_params=pltpu.CompilerParams(vmem_limit_bytes=GRANT),
        cost_estimate=SMALL,
    )(*parts)


def on_device(embeddings, cluster_ids, order_rank):
    unit = payload(embeddings, cluster_ids, order_rank)
    mine, theirs = {0: join(unit, swap(unit))}, {}
    near, far = (0, 1, 2, 4), (3, 6, 5)
    for m in (1, 2, 4):
        mine[m] = exchange(mine[0], m)
    mine[3] = exchange(mine[1], 2)
    mine[6] = exchange(mine[2], 4)
    mine[5] = exchange(mine[4], 1)
    theirs.update({m: swap(pack(mine[m])[0]) for m in (1, 2, 4)})
    mine[7] = exchange(mine[3], 4)
    theirs.update({m: swap(pack(mine[m])[0]) for m in far})
    every = (*near, *far, 7)
    best = match((4, 6, 5), near, mine, theirs)
    best = match((4, 6, 5), far, mine, theirs, best)
    part = match((2, 3), near, mine, theirs)
    part, best, mine[7] = lax.optimization_barrier((part, best, mine[7]))
    theirs[7] = swap(pack(mine[7])[0])
    best = match((7,), (*near, *far), mine, theirs, best)
    send = match((4, 6, 5, 7), (7,), mine, theirs, best, last=True)
    send, mine[0] = lax.optimization_barrier((send, mine[0]))
    first = exchange(send, 4)
    send = fold(2, match((2, 3), (*far, 7), mine, theirs, part), first)
    send, mine[0] = lax.optimization_barrier((send, mine[0]))
    second = exchange(send, 2)
    send = fold(1, match((1,), every, mine, theirs), first, second)
    send, mine[0] = lax.optimization_barrier((send, mine[0]))
    third = exchange(send, 1)
    return fold(0, match((0,), every, mine, theirs), first, second, third).reshape(ROWS)


def solution(mesh):
    return jax.shard_map(
        on_device,
        mesh=mesh,
        in_specs=(P(AXES, None), P(AXES, None), P(AXES)),
        out_specs=P(AXES),
        check_vma=False,
    )
```

```python
import functools

import jax
import jax.numpy as jnp
from jax import lax
from jax.experimental import pallas as pl
from jax.experimental.pallas import tpu as pltpu
from jax.sharding import PartitionSpec as P

AXES = ("group", "tile")
ROWS = 256
META = 16
PIECES = 2
PAY = ROWS + META
E = 512
LOW = -(2**31)
GRANT = 12 * 2**20
SMALL = pl.CostEstimate(flops=1000, bytes_accessed=1000, transcendentals=0)
NEAR = (1, 0, 3, 2)
OTHER = (3, 2, 1, 0)
PLACES = [(x, y, z, c) for x in range(4) for y in range(4) for z in range(4) for c in range(2)]


def linear(x, y, z, c):
    return (z * 2 + c) * 16 + y * 4 + x


def across(place, mask):
    x, y, z, c = place
    step = OTHER if c else NEAR
    return (
        step[x] if mask & 1 else x,
        step[y] if mask & 2 else y,
        step[z] if mask & 4 else z,
        c,
    )


def exchange(array, mask):
    pairs = [(linear(*across(q, mask)), linear(*q)) for q in PLACES]
    return lax.ppermute(array, AXES, pairs)


def swap(array):
    pairs = [(linear(x, y, z, 1 - c), linear(x, y, z, c)) for x, y, z, c in PLACES]
    return lax.ppermute(array, AXES, pairs)


def unit_kernel(emb_hbm, cluster_hbm, rank_hbm, out_ref, emb_ref, cluster_ref, rank_ref, sem):
    small = [
        pltpu.make_async_copy(cluster_hbm, cluster_ref, sem.at[PIECES]),
        pltpu.make_async_copy(rank_hbm, rank_ref, sem.at[PIECES + 1]),
    ]
    size = ROWS // PIECES
    pieces = [pl.ds(i * size, size) for i in range(PIECES)]
    large = [pltpu.make_async_copy(emb_hbm.at[p], emb_ref.at[p], sem.at[i]) for i, p in enumerate(pieces)]
    for copy in large + small:
        copy.start()
    for piece, copy in zip(pieces, large):
        copy.wait()
        emb = emb_ref[piece, :]
        sums = jnp.sum(emb * emb, axis=1, keepdims=True)
        out_ref[piece, :] = (emb * lax.rsqrt(sums + 1e-06)).astype(jnp.bfloat16)
    for copy in small:
        copy.wait()
    rank = rank_ref[...]
    high = (rank >> 8).astype(jnp.float32)
    low = (rank & 255).astype(jnp.float32)
    cluster = cluster_ref[...].astype(jnp.float32)
    first = jnp.concatenate([high, low], axis=1)
    second = jnp.concatenate([cluster, jnp.zeros_like(cluster)], axis=1)
    row = lax.broadcasted_iota(jnp.int32, (META, E), 0)
    meta = jnp.where(row == 0, first, jnp.where(row == 1, second, 0.0))
    out_ref[ROWS:PAY, :] = meta.astype(jnp.bfloat16)


def payload(embeddings, cluster_ids, order_rank):
    outside = pl.BlockSpec(memory_space=pltpu.HBM)
    return pl.pallas_call(
        unit_kernel,
        out_shape=jax.ShapeDtypeStruct((PAY, E), jnp.bfloat16),
        in_specs=[outside] * 3,
        out_specs=pl.BlockSpec(memory_space=pltpu.VMEM),
        scratch_shapes=[
            pltpu.VMEM((ROWS, E), jnp.float32),
            pltpu.VMEM((1, ROWS), jnp.int32),
            pltpu.VMEM((1, ROWS), jnp.int32),
            pltpu.SemaphoreType.DMA((PIECES + 2,)),
        ],
        compiler_params=pltpu.CompilerParams(vmem_limit_bytes=GRANT),
        cost_estimate=SMALL,
    )(*[pltpu.with_memory_space_constraint(x, pltpu.HBM) for x in (embeddings, cluster_ids.reshape(1, ROWS), order_rank.reshape(1, ROWS))])


def join_kernel(first_ref, second_ref, out_ref):
    out_ref[0] = first_ref[...]
    out_ref[1] = second_ref[...]


def join(first, second):
    vmem = pl.BlockSpec(memory_space=pltpu.VMEM)
    return pl.pallas_call(
        join_kernel,
        out_shape=jax.ShapeDtypeStruct((2, PAY, E), jnp.bfloat16),
        in_specs=[vmem] * 2,
        out_specs=vmem,
        compiler_params=pltpu.CompilerParams(vmem_limit_bytes=GRANT),
        cost_estimate=SMALL,
    )(first, second)


def pack_kernel(*refs):
    half = len(refs) // 2
    for source, out in zip(refs[:half], refs[half:]):
        out[0:ROWS, :] = source[0, 0:ROWS, :]
        out[ROWS : 2 * ROWS, :] = source[1, 0:ROWS, :]
        one = source[0, ROWS:PAY, :].astype(jnp.float32)
        two = source[1, ROWS:PAY, :].astype(jnp.float32)
        both = jnp.concatenate([one[0:2], two[0:2], jnp.zeros((META - 4, E), jnp.float32)], axis=0)
        out[2 * ROWS : 2 * ROWS + META, :] = both.astype(jnp.bfloat16)


def pack(*blocks):
    vmem = pl.BlockSpec(memory_space=pltpu.VMEM)
    return pl.pallas_call(
        pack_kernel,
        out_shape=[jax.ShapeDtypeStruct((2 * ROWS + META, E), jnp.bfloat16)] * len(blocks),
        in_specs=[vmem] * len(blocks),
        out_specs=[vmem] * len(blocks),
        compiler_params=pltpu.CompilerParams(vmem_limit_bytes=GRANT),
        cost_estimate=SMALL,
    )(*blocks)


def match_kernel(queries, keys, masks, begin, last, *refs):
    mine = dict(zip(masks, refs[0 : len(masks)]))
    others = [n for n in keys if n]
    theirs = dict(zip(others, refs[len(masks) : len(masks) + len(others)]))
    out_ref, first, second = refs[-3:]

    def numbers(meta, at):
        rank = meta[at : at + 1, 0:ROWS] * 256.0 + meta[at : at + 1, ROWS : 2 * ROWS]
        return rank, meta[at + 1 : at + 2, 0:ROWS] * 32768.0 + rank

    def columns(row):
        return jnp.broadcast_to(jnp.transpose(jnp.broadcast_to(row, (8, ROWS)))[:, 0:1], (ROWS, 128)).astype(jnp.int32)

    def product(left, right):
        return lax.dot_general(left, right, (((1,), (1,)), ((), ())), preferred_element_type=jnp.float32)

    def ask(m):
        return mine[m][0, 0:ROWS, :]

    def give(n, h):
        return theirs[n][h * ROWS : h * ROWS + ROWS, :] if n else mine[0][h, 0:ROWS, :]

    def given(n, h):
        meta = theirs[n][2 * ROWS : 2 * ROWS + META, :] if n else mine[0][h, ROWS:PAY, :]
        return numbers(meta.astype(jnp.float32), 2 * h if n else 0)[1]

    found = {}
    sides = [(n, h) for n in keys for h in range(2)]
    limits = {m: numbers(mine[m][0, ROWS:PAY, :].astype(jnp.float32), 0) for m in queries}
    wanted = {side: given(*side) for side in sides}
    if len(queries) < len(keys):
        for i, m in enumerate(queries):
            first[i] = columns(limits[m][1])
            second[i] = columns(limits[m][0]) + LOW
        rows = {side: wanted[side].astype(jnp.int32) + (LOW + 1) for side in sides}
        for i, m in enumerate(queries):
            best = jnp.full((ROWS, 128), -1.0, jnp.float32)
            for side in sides:
                score = product(ask(m), give(*side))
                for lanes in (slice(0, 128), slice(128, 256)):
                    valid = first[i] - rows[side][:, lanes] < second[i]
                    best = jnp.maximum(best, jnp.where(valid, score[:, lanes], -1.0))
            found[m] = jnp.max(jnp.transpose(best), axis=0, keepdims=True)
    else:
        for i, side in enumerate(sides):
            first[i] = columns(wanted[side]) + (LOW + 1)
        for m in queries:
            row = jnp.broadcast_to(limits[m][1].astype(jnp.int32), (8, ROWS))
            limit = jnp.broadcast_to(limits[m][0].astype(jnp.int32) + LOW, (8, ROWS))
            best = jnp.full((8, ROWS), -1.0, jnp.float32)
            for i, side in enumerate(sides):
                score = product(give(*side), ask(m))
                for r in range(0, ROWS, 8):
                    column = first[i, r : r + 8, :]
                    valid = row - jnp.concatenate([column, column], axis=1) < limit
                    best = jnp.maximum(best, jnp.where(valid, score[r : r + 8, :], -1.0))
            found[m] = jnp.max(best, axis=0, keepdims=True)
    old = None if begin else refs[-4]
    skip = 4 if last else 0
    for m in range(skip, 8):
        best = jnp.full((1, ROWS), -1.0, jnp.float32) if begin else old[m]
        best = jnp.maximum(best, found[m]) if m in found else best
        out_ref[m - skip] = best


def match(queries, keys, mine, theirs, *prev, last=False):
    masks = sorted(set(queries) | ({0} & set(keys)))
    others = [n for n in keys if n]
    columns = len(queries) if len(queries) < len(keys) else 2 * len(keys)
    vmem = pl.BlockSpec(memory_space=pltpu.VMEM)
    return pl.pallas_call(
        functools.partial(match_kernel, queries, keys, masks, not prev, last),
        out_shape=jax.ShapeDtypeStruct((4 if last else 8, 1, ROWS), jnp.float32),
        in_specs=[vmem] * (len(masks) + len(others) + len(prev)),
        out_specs=vmem,
        scratch_shapes=[pltpu.VMEM((columns, ROWS, 128), jnp.int32)] * 2,
        compiler_params=pltpu.CompilerParams(vmem_limit_bytes=GRANT),
        cost_estimate=SMALL,
    )(*[mine[m] for m in masks], *[theirs[n] for n in others], *prev)


def fold_kernel(row, *refs):
    out_ref = refs[-1]
    total = refs[0][row : row + 1] if row < 2 else refs[0][row : row + 2]
    for come_ref in refs[1:-1]:
        total = jnp.maximum(total, come_ref[row : row + total.shape[0]])
    out_ref[...] = total if row else total[0]


def fold(row, *parts):
    vmem = pl.BlockSpec(memory_space=pltpu.VMEM)
    shape = {0: (1, ROWS), 1: (1, 1, ROWS), 2: (2, 1, ROWS)}[row]
    return pl.pallas_call(
        functools.partial(fold_kernel, row),
        out_shape=jax.ShapeDtypeStruct(shape, jnp.float32),
        in_specs=[vmem] * len(parts),
        out_specs=vmem,
        compiler_params=pltpu.CompilerParams(vmem_limit_bytes=GRANT),
        cost_estimate=SMALL,
    )(*parts)


def on_device(embeddings, cluster_ids, order_rank):
    unit = payload(embeddings, cluster_ids, order_rank)
    mine, theirs = {0: join(unit, swap(unit))}, {}
    near, far = (0, 1, 2, 4), (3, 6, 5)
    for m in (1, 2, 4):
        mine[m] = exchange(mine[0], m)
    mine[3] = exchange(mine[1], 2)
    mine[6] = exchange(mine[2], 4)
    mine[5] = exchange(mine[4], 1)
    theirs.update({m: swap(pack(mine[m])[0]) for m in (1, 2, 4)})
    mine[7] = exchange(mine[3], 4)
    theirs.update({m: swap(pack(mine[m])[0]) for m in far})
    every = (*near, *far, 7)
    best = match((4, 6, 5), near, mine, theirs)
    best = match((4, 6, 5), far, mine, theirs, best)
    part = match((2, 3), near, mine, theirs)
    part, best, mine[7] = lax.optimization_barrier((part, best, mine[7]))
    theirs[7] = swap(pack(mine[7])[0])
    best = match((7,), (*near, *far), mine, theirs, best)
    send = match((4, 6, 5, 7), (7,), mine, theirs, best, last=True)
    send, mine[0] = lax.optimization_barrier((send, mine[0]))
    first = exchange(send, 4)
    send = fold(2, match((2, 3), (*far, 7), mine, theirs, part), first)
    send, mine[0] = lax.optimization_barrier((send, mine[0]))
    second = exchange(send, 2)
    send = fold(1, match((1,), every, mine, theirs), first, second)
    send, mine[0] = lax.optimization_barrier((send, mine[0]))
    third = exchange(send, 1)
    return fold(0, match((0,), every, mine, theirs), first, second, third).reshape(ROWS)


def solution(mesh):
    return jax.shard_map(
        on_device,
        mesh=mesh,
        in_specs=(P(AXES, None), P(AXES, None), P(AXES)),
        out_specs=P(AXES),
        check_vma=False,
    )
```

```python
import functools

import jax
import jax.numpy as jnp
from jax import lax
from jax.experimental import pallas as pl
from jax.experimental.pallas import tpu as pltpu
from jax.sharding import PartitionSpec as P

AXES = ("group", "tile")
ROWS = 256
META = 16
PAY = ROWS + META
E = 512
LOW = -(2**31)
GRANT = 12 * 2**20
SMALL = pl.CostEstimate(flops=1000, bytes_accessed=1000, transcendentals=0)
NEAR = (1, 0, 3, 2)
OTHER = (3, 2, 1, 0)
PLACES = [(x, y, z, c) for x in range(4) for y in range(4) for z in range(4) for c in range(2)]


def linear(x, y, z, c):
    return (z * 2 + c) * 16 + y * 4 + x


def across(place, mask):
    x, y, z, c = place
    step = OTHER if c else NEAR
    return (
        step[x] if mask & 1 else x,
        step[y] if mask & 2 else y,
        step[z] if mask & 4 else z,
        c,
    )


def exchange(array, mask):
    pairs = [(linear(*across(q, mask)), linear(*q)) for q in PLACES]
    return lax.ppermute(array, AXES, pairs)


def swap(array):
    pairs = [(linear(x, y, z, 1 - c), linear(x, y, z, c)) for x, y, z, c in PLACES]
    return lax.ppermute(array, AXES, pairs)


def unit_kernel(emb_hbm, cluster_hbm, rank_hbm, out_ref, emb_ref, cluster_ref, rank_ref, sem):
    sources = (cluster_hbm, rank_hbm, emb_hbm)
    targets = (cluster_ref, rank_ref, emb_ref)
    copies = [pltpu.make_async_copy(a, b, sem.at[i]) for i, (a, b) in enumerate(zip(sources, targets))]
    for copy in copies:
        copy.start()
    for copy in copies:
        copy.wait()
    emb = emb_ref[...]
    sums = jnp.sum(emb * emb, axis=1, keepdims=True)
    out_ref[0:ROWS, :] = (emb * lax.rsqrt(sums + 1e-06)).astype(jnp.bfloat16)
    rank = rank_ref[...]
    high = (rank >> 8).astype(jnp.float32)
    low = (rank & 255).astype(jnp.float32)
    cluster = cluster_ref[...].astype(jnp.float32)
    first = jnp.concatenate([high, low], axis=1)
    second = jnp.concatenate([cluster, jnp.zeros_like(cluster)], axis=1)
    row = lax.broadcasted_iota(jnp.int32, (META, E), 0)
    meta = jnp.where(row == 0, first, jnp.where(row == 1, second, 0.0))
    out_ref[ROWS:PAY, :] = meta.astype(jnp.bfloat16)


def payload(embeddings, cluster_ids, order_rank):
    outside = pl.BlockSpec(memory_space=pltpu.HBM)
    return pl.pallas_call(
        unit_kernel,
        out_shape=jax.ShapeDtypeStruct((PAY, E), jnp.bfloat16),
        in_specs=[outside] * 3,
        out_specs=pl.BlockSpec(memory_space=pltpu.VMEM),
        scratch_shapes=[
            pltpu.VMEM((ROWS, E), jnp.float32),
            pltpu.VMEM((1, ROWS), jnp.int32),
            pltpu.VMEM((1, ROWS), jnp.int32),
            pltpu.SemaphoreType.DMA((3,)),
        ],
        compiler_params=pltpu.CompilerParams(vmem_limit_bytes=GRANT),
        cost_estimate=SMALL,
    )(*[pltpu.with_memory_space_constraint(x, pltpu.HBM) for x in (embeddings, cluster_ids.reshape(1, ROWS), order_rank.reshape(1, ROWS))])


def join_kernel(first_ref, second_ref, out_ref):
    out_ref[0] = first_ref[...]
    out_ref[1] = second_ref[...]


def join(first, second):
    vmem = pl.BlockSpec(memory_space=pltpu.VMEM)
    return pl.pallas_call(
        join_kernel,
        out_shape=jax.ShapeDtypeStruct((2, PAY, E), jnp.bfloat16),
        in_specs=[vmem] * 2,
        out_specs=vmem,
        compiler_params=pltpu.CompilerParams(vmem_limit_bytes=GRANT),
        cost_estimate=SMALL,
    )(first, second)


def pack_kernel(*refs):
    half = len(refs) // 2
    for source, out in zip(refs[:half], refs[half:]):
        out[0:ROWS, :] = source[0, 0:ROWS, :]
        out[ROWS : 2 * ROWS, :] = source[1, 0:ROWS, :]
        one = source[0, ROWS:PAY, :].astype(jnp.float32)
        two = source[1, ROWS:PAY, :].astype(jnp.float32)
        both = jnp.concatenate([one[0:2], two[0:2], jnp.zeros((META - 4, E), jnp.float32)], axis=0)
        out[2 * ROWS : 2 * ROWS + META, :] = both.astype(jnp.bfloat16)


def pack(*blocks):
    vmem = pl.BlockSpec(memory_space=pltpu.VMEM)
    return pl.pallas_call(
        pack_kernel,
        out_shape=[jax.ShapeDtypeStruct((2 * ROWS + META, E), jnp.bfloat16)] * len(blocks),
        in_specs=[vmem] * len(blocks),
        out_specs=[vmem] * len(blocks),
        compiler_params=pltpu.CompilerParams(vmem_limit_bytes=GRANT),
        cost_estimate=SMALL,
    )(*blocks)


def match_kernel(queries, keys, masks, begin, last, *refs):
    mine = dict(zip(masks, refs[0 : len(masks)]))
    others = [n for n in keys if n]
    theirs = dict(zip(others, refs[len(masks) : len(masks) + len(others)]))
    out_ref, first, second = refs[-3:]

    def numbers(meta, at):
        rank = meta[at : at + 1, 0:ROWS] * 256.0 + meta[at : at + 1, ROWS : 2 * ROWS]
        return rank, meta[at + 1 : at + 2, 0:ROWS] * 32768.0 + rank

    def columns(row):
        return jnp.broadcast_to(jnp.transpose(jnp.broadcast_to(row, (8, ROWS)))[:, 0:1], (ROWS, 128)).astype(jnp.int32)

    def product(left, right):
        return lax.dot_general(left, right, (((1,), (1,)), ((), ())), preferred_element_type=jnp.float32)

    def ask(m):
        return mine[m][0, 0:ROWS, :]

    def give(n, h):
        return theirs[n][h * ROWS : h * ROWS + ROWS, :] if n else mine[0][h, 0:ROWS, :]

    def given(n, h):
        meta = theirs[n][2 * ROWS : 2 * ROWS + META, :] if n else mine[0][h, ROWS:PAY, :]
        return numbers(meta.astype(jnp.float32), 2 * h if n else 0)[1]

    found = {}
    sides = [(n, h) for n in keys for h in range(2)]
    limits = {m: numbers(mine[m][0, ROWS:PAY, :].astype(jnp.float32), 0) for m in queries}
    wanted = {side: given(*side) for side in sides}
    if len(queries) < len(keys):
        for i, m in enumerate(queries):
            first[i] = columns(limits[m][1])
            second[i] = columns(limits[m][0]) + LOW
        rows = {side: wanted[side].astype(jnp.int32) + (LOW + 1) for side in sides}
        for i, m in enumerate(queries):
            best = jnp.full((ROWS, 128), -1.0, jnp.float32)
            for side in sides:
                score = product(ask(m), give(*side))
                for lanes in (slice(0, 128), slice(128, 256)):
                    valid = first[i] - rows[side][:, lanes] < second[i]
                    best = jnp.maximum(best, jnp.where(valid, score[:, lanes], -1.0))
            found[m] = jnp.max(jnp.transpose(best), axis=0, keepdims=True)
    else:
        for i, side in enumerate(sides):
            first[i] = columns(wanted[side]) + (LOW + 1)
        for m in queries:
            row = jnp.broadcast_to(limits[m][1].astype(jnp.int32), (8, ROWS))
            limit = jnp.broadcast_to(limits[m][0].astype(jnp.int32) + LOW, (8, ROWS))
            best = jnp.full((8, ROWS), -1.0, jnp.float32)
            for i, side in enumerate(sides):
                score = product(give(*side), ask(m))
                for r in range(0, ROWS, 8):
                    column = first[i, r : r + 8, :]
                    valid = row - jnp.concatenate([column, column], axis=1) < limit
                    best = jnp.maximum(best, jnp.where(valid, score[r : r + 8, :], -1.0))
            found[m] = jnp.max(best, axis=0, keepdims=True)
    old = None if begin else refs[-4]
    skip = 4 if last else 0
    for m in range(skip, 8):
        best = jnp.full((1, ROWS), -1.0, jnp.float32) if begin else old[m]
        best = jnp.maximum(best, found[m]) if m in found else best
        out_ref[m - skip] = best


def match(queries, keys, mine, theirs, *prev, last=False):
    masks = sorted(set(queries) | ({0} & set(keys)))
    others = [n for n in keys if n]
    columns = len(queries) if len(queries) < len(keys) else 2 * len(keys)
    vmem = pl.BlockSpec(memory_space=pltpu.VMEM)
    return pl.pallas_call(
        functools.partial(match_kernel, queries, keys, masks, not prev, last),
        out_shape=jax.ShapeDtypeStruct((4 if last else 8, 1, ROWS), jnp.float32),
        in_specs=[vmem] * (len(masks) + len(others) + len(prev)),
        out_specs=vmem,
        scratch_shapes=[pltpu.VMEM((columns, ROWS, 128), jnp.int32)] * 2,
        compiler_params=pltpu.CompilerParams(vmem_limit_bytes=GRANT),
        cost_estimate=SMALL,
    )(*[mine[m] for m in masks], *[theirs[n] for n in others], *prev)


def fold_kernel(row, *refs):
    out_ref = refs[-1]
    total = refs[0][row : row + 1] if row < 2 else refs[0][row : row + 2]
    for come_ref in refs[1:-1]:
        total = jnp.maximum(total, come_ref[row : row + total.shape[0]])
    out_ref[...] = total if row else total[0]


def fold(row, *parts):
    vmem = pl.BlockSpec(memory_space=pltpu.VMEM)
    shape = {0: (1, ROWS), 1: (1, 1, ROWS), 2: (2, 1, ROWS)}[row]
    return pl.pallas_call(
        functools.partial(fold_kernel, row),
        out_shape=jax.ShapeDtypeStruct(shape, jnp.float32),
        in_specs=[vmem] * len(parts),
        out_specs=vmem,
        compiler_params=pltpu.CompilerParams(vmem_limit_bytes=GRANT),
        cost_estimate=SMALL,
    )(*parts)


def on_device(embeddings, cluster_ids, order_rank):
    unit = payload(embeddings, cluster_ids, order_rank)
    mine, theirs = {0: join(unit, swap(unit))}, {}
    near, far = (0, 1, 2, 4), (3, 6, 5)
    for m in (1, 2, 4):
        mine[m] = exchange(mine[0], m)
    mine[3] = exchange(mine[1], 2)
    mine[6] = exchange(mine[2], 4)
    mine[5] = exchange(mine[4], 1)
    theirs.update({m: swap(pack(mine[m])[0]) for m in (1, 2, 4)})
    mine[7] = exchange(mine[3], 4)
    theirs.update({m: swap(pack(mine[m])[0]) for m in far})
    every = (*near, *far, 7)
    best = match((4, 6, 5), near, mine, theirs)
    best = match((4, 6, 5), far, mine, theirs, best)
    part = match((2,), near, mine, theirs)
    part, best, mine[7] = lax.optimization_barrier((part, best, mine[7]))
    theirs[7] = swap(pack(mine[7])[0])
    best = match((7,), (*near, *far), mine, theirs, best)
    send = match((4, 6, 5, 7), (7,), mine, theirs, best, last=True)
    send, mine[0] = lax.optimization_barrier((send, mine[0]))
    first = exchange(send, 4)
    part = match((3,), near, mine, theirs, part)
    send = fold(2, match((2, 3), (*far, 7), mine, theirs, part), first)
    send, mine[0] = lax.optimization_barrier((send, mine[0]))
    second = exchange(send, 2)
    send = fold(1, match((1,), every, mine, theirs), first, second)
    send, mine[0] = lax.optimization_barrier((send, mine[0]))
    third = exchange(send, 1)
    return fold(0, match((0,), every, mine, theirs), first, second, third).reshape(ROWS)


def solution(mesh):
    return jax.shard_map(
        on_device,
        mesh=mesh,
        in_specs=(P(AXES, None), P(AXES, None), P(AXES)),
        out_specs=P(AXES),
        check_vma=False,
    )
```
